256 devices in a mesh: rows: 128 (over x, y, z), grp: 2 (over core).
Axes of the slice: x: 4, y: 4, z: 8, core: 2. Of those that a mesh axis runs over, the one named last changes fastest.
Arguments:
- features: float32 [131072, 128], P(('rows', 'grp')), may hold values from -6 to 6
- weight: float32 [128, 256], replicated, may hold values from -0.5 to 0.5
- bias: float32 [256], replicated, may hold values from -3 to 3
- cotangent: float32 [131072, 256], P(('rows', 'grp')), may hold values from -6 to 6
- loc_vals: float32 [131072, 256], P(('rows', 'grp')), may hold values from -0.21875 to 0.21875
- loc_cols: int32 [2048, 4], P(('rows', 'grp')), may hold values from 0 to 7, as said below
- loc_count: int32 [2048], P(('rows', 'grp')), may hold values from 1 to 4, as said below
- hub_rows: int32 [1024], P(('rows', 'grp')), may hold values from 0 to 511, as said below
- hub_vals: float32 [131072, 1024], P(('rows', 'grp')), may hold values from -0.109375 to 0.109375
- send_rows: int32 [256, 128, 4], P(('rows', 'grp')), may hold values from 0 to 511, as said below
- bnd_vals: float32 [131072, 512], P(('rows', 'grp')), may hold values from -0.15625 to 0.15625
Outputs:
- activation: float32 [131072, 256], P(('rows', 'grp'))
- weight_grad: float32 [128, 256], replicated
- feat_grad: float32 [131072, 128], P(('rows', 'grp'))
The draws below stay inside these ranges and needn't reach their ends.
Inputs may be any that keep to these rules, and one draw needn't show every extreme that they name: `loc_cols`: the 4 listed column tiles of one row tile are distinct. The first loc_count listed tiles of a row tile are live, the others are ignored. `hub_rows`: the 4 hub rows of one device are distinct. `send_rows`: the 4 rows that one device sends to one rows index are distinct.
All inputs are finite; a program needn't handle non-finite values.
Results may differ from the reference program's by a relative error of at most 0.0003.
Values sent between devices are 32-bit elements; how exact they have to be, the bound alone decides.
A program may use at most 64 MiB of HBM per device.

```python
import jax
import jax.numpy as jnp
from jax import lax

F = 128
H = 256
NODE_DEV = 512
HUB_DEV = 4
BND = 4
TB = 64
KT = 4
NODES = 131072
HUBS = 1024
N_ROWS = 128
N_GRP = 2
DEVICES = 256


def draw_hub_rows(key, part):
    key = jax.random.fold_in(key, 11)
    first, second = jax.random.split(key, 2)
    band = NODE_DEV // HUB_DEV
    offsets = jax.random.randint(first, (DEVICES, HUB_DEV), 0, band)
    chosen = jax.random.randint(second, (2,), 0, DEVICES)
    device_ids = jnp.arange(DEVICES)[:, None]
    slots = jnp.arange(HUB_DEV)[None, :]
    offsets = jnp.where((device_ids == chosen[0]) & (slots == HUB_DEV - 1), band - 1, offsets)
    offsets = jnp.where((device_ids == chosen[1]) & (slots == 0), 0, offsets)
    return (slots * band + offsets).reshape(-1).astype(jnp.int32)


def draw_send_rows(key, part):
    key = jax.random.fold_in(key, 23)
    first, second = jax.random.split(key, 2)
    band = NODE_DEV // BND
    offsets = jax.random.randint(first, (DEVICES, N_ROWS, BND), 0, band)
    chosen = jax.random.randint(second, (2,), 0, DEVICES)
    device_ids = jnp.arange(DEVICES)[:, None, None]
    slots = jnp.arange(BND)[None, None, :]
    offsets = jnp.where((device_ids == chosen[0]) & (slots == BND - 1), band - 1, offsets)
    offsets = jnp.where((device_ids == chosen[1]) & (slots == 0), 0, offsets)
    return (slots * band + offsets).astype(jnp.int32)


def draw_loc_cols(key, part):
    key = jax.random.fold_in(key, 37)
    tiles_dev = NODE_DEV // TB
    scores = jax.random.randint(key, (DEVICES * tiles_dev, tiles_dev), 0, 2 ** 20)
    scores = scores * tiles_dev + jnp.arange(tiles_dev)[None, :]
    picked = jax.lax.top_k(scores, KT)[1]
    return picked.astype(jnp.int32)


def draw_loc_count(key, part):
    key = jax.random.fold_in(key, 41)
    first, second, third = jax.random.split(key, 3)
    tiles_dev = NODE_DEV // TB
    level = jax.random.randint(first, (DEVICES,), 0, 2)
    extra = jax.random.randint(second, (DEVICES, tiles_dev), 0, 2)
    count = 1 + extra * level[:, None]
    chosen = jax.random.randint(third, (), 0, DEVICES)
    device_ids = jnp.arange(DEVICES)[:, None]
    count = jnp.where(device_ids == chosen, KT, count)
    return count.reshape(-1).astype(jnp.int32)


def block_levels(rng, extent, cuts, least, largest):
    factor_of = 1.0
    for dim, blocks in cuts:
        steps = jax.random.uniform(jax.random.fold_in(jax.random.fold_in(rng, 6), dim), (blocks,), jnp.float32, least / len(cuts), largest / len(cuts))
        factor_of = factor_of * jnp.repeat(jnp.exp(steps), extent[dim] // blocks).reshape((-1,) + (1,) * (len(extent) - 1 - dim))
    return factor_of


def centred(rng, extent, spread, most, cuts=(), kind=jnp.bfloat16):
    entries = jax.random.normal(rng, extent, jnp.float32) * spread
    if len(cuts) > 0:
        entries = block_levels(rng, extent, cuts, -0.22, 0.18) * entries
    return jnp.clip(entries, min=-most, max=most).astype(kind)


def setup_inputs(seed: int = 0) -> dict:
    splits = jax.random.split(jax.random.key(seed), 12)
    return {
        "features": centred(splits[0], (NODES, F), 1.0, 6.0, ((0, 256),), jnp.float32),
        "weight": centred(splits[1], (F, H), F ** -0.5, 0.5, (), jnp.float32),
        "bias": centred(splits[2], (H,), 0.5, 3.0, (), jnp.float32),
        "cotangent": centred(splits[3], (NODES, H), 1.0, 6.0, ((0, 256),), jnp.float32),
        "loc_vals": centred(splits[4], (NODES, KT * TB), (3 * KT * TB) ** -0.5, 0.21875, ((0, 256),), jnp.float32),
        "loc_cols": draw_loc_cols(jax.random.fold_in(splits[11], 71), 0),
        "loc_count": draw_loc_count(jax.random.fold_in(splits[11], 71), 0),
        "hub_rows": draw_hub_rows(jax.random.fold_in(splits[11], 71), 0),
        "hub_vals": centred(splits[8], (NODES, HUBS), (3 * HUBS) ** -0.5, 0.109375, ((0, 256),), jnp.float32),
        "send_rows": draw_send_rows(jax.random.fold_in(splits[11], 71), 0),
        "bnd_vals": centred(splits[10], (NODES, N_ROWS * BND), (3 * N_ROWS * BND) ** -0.5, 0.15625, ((0, 256),), jnp.float32),
    }


def gelu_tanh(value):
    return jax.nn.gelu(value, approximate=True)

def aggregate(features, loc_vals, loc_cols, loc_count, hub_rows, hub_vals, send_rows, bnd_vals):
    highest = lax.Precision.HIGHEST
    tiles_dev = NODE_DEV // TB
    device_ids = jnp.arange(DEVICES, dtype=jnp.int32)
    hub_ids = (device_ids[:, None] * NODE_DEV + hub_rows.reshape(DEVICES, HUB_DEV)).reshape(-1)
    hub_feat = features[hub_ids]
    blocks = features.reshape(DEVICES, tiles_dev, TB, F)
    local_vals = loc_vals.reshape(DEVICES, tiles_dev, TB, KT, TB)
    local_cols = loc_cols.reshape(DEVICES, tiles_dev, KT)
    local_count = loc_count.reshape(DEVICES, tiles_dev)
    hub_block = hub_vals.reshape(DEVICES, NODE_DEV, HUBS)
    bnd_block = bnd_vals.reshape(DEVICES, NODE_DEV, N_ROWS * BND)

    def one_device(items):
        device, block, vals, cols, count, hub_part, bnd_part = items
        row_index = device // N_GRP
        grp_index = device % N_GRP
        sources = jnp.arange(N_ROWS, dtype=jnp.int32) * N_GRP + grp_index
        sent = send_rows[sources, row_index]
        node_ids = (sources[:, None] * NODE_DEV + sent).reshape(-1)
        bnd_feat = features[node_ids]
        picked = block[cols]
        live = (jnp.arange(KT, dtype=jnp.int32)[None, :] < count[:, None]).astype(jnp.float32)
        picked = picked * live[:, :, None, None]
        local_sum = jnp.einsum('tikj,tkjf->tif', vals, picked, precision=highest).reshape(NODE_DEV, F)
        hub_sum = jnp.dot(hub_part, hub_feat, precision=highest)
        bnd_sum = jnp.dot(bnd_part, bnd_feat, precision=highest)
        return local_sum + hub_sum + bnd_sum
    result = lax.map(one_device, (device_ids, blocks, local_vals, local_cols, local_count, hub_block, bnd_block))
    return result.reshape(NODES, F)

def reference(features, weight, bias, cotangent, loc_vals, loc_cols, loc_count, hub_rows, hub_vals, send_rows, bnd_vals):
    highest = lax.Precision.HIGHEST

    def apply_graph(field):
        return aggregate(field, loc_vals, loc_cols, loc_count, hub_rows, hub_vals, send_rows, bnd_vals)
    aggregated, graph_pull = jax.vjp(apply_graph, features)
    pre = jnp.dot(aggregated, weight, precision=highest) + bias
    activation, act_pull = jax.vjp(gelu_tanh, pre)
    pre_grad = act_pull(cotangent)[0]
    weight_grad = jnp.dot(aggregated.T, pre_grad, precision=highest) * NODES ** (-0.5)
    aggregated_grad = jnp.dot(pre_grad, weight.T, precision=highest)
    feat_grad = graph_pull(aggregated_grad)[0]
    return (activation, weight_grad, feat_grad)
```

```python
import functools
import math

import jax
import jax.numpy as jnp
from jax import lax
from jax.experimental import pallas as pl
from jax.experimental.pallas import tpu as pltpu
from jax.sharding import PartitionSpec as P

TB = 64
KT = 4
MESH = pl.DeviceIdType.MESH
F32 = jnp.float32
BF16 = jnp.bfloat16
C0 = math.sqrt(2.0 / math.pi)
C1 = 0.044715


def split(value):
    high = value.astype(BF16)
    low = (value - high.astype(F32)).astype(BF16)
    return high, low


def mm(left, right):
    return jnp.dot(left, right, preferred_element_type=F32)


def wide(value):
    high, low = split(value)
    return jnp.concatenate([high, low], axis=1)


def mm3(high, low, pair):
    n = pair.shape[1] // 2
    both = mm(high, pair)
    return both[:, :n] + both[:, n:] + mm(low, pair[:, :n])


def kernel(
    XY, Z,
    feat_h, w_h, b_h, cot_h, lv_h, lcols_h, lcount_h, hrows_h, hv_h, srows_h, bv_h,
    act_o, wg_o, fg_o,
    feat, w, b, cot, lv, lcols, lcount, hrows, hrows_v, hv, srows, srows_v, bv,
    ahi, alo, athi, atlo, wt, wpair,
    hown, s1, r1, h1, br, hub,
    agg, prg, dag,
    gs, gsib, gown, gx, gp, gz,
    bsend, bx, ar,
    ws, wx, wp, wz, wsum, wsib, wall,
    in_sem, loc_sem, ssem, rsem,
):
    r = lax.axis_index("rows")
    g = lax.axis_index("grp")
    xy = r // Z
    z = lax.rem(r, Z)
    half = Z // 2
    R = XY * Z
    F = feat.shape[1]
    N = feat.shape[0]
    nb = bv.shape[1]
    nh = hv.shape[1]
    hb = half * 8

    loads = {}
    for i, (name, src, dst) in enumerate([
        ("feat", feat_h, feat), ("srows", srows_h, srows), ("hrows", hrows_h, hrows),
        ("lcols", lcols_h, lcols), ("lcount", lcount_h, lcount),
        ("lv", lv_h, lv), ("bv", bv_h, bv), ("hv", hv_h, hv), ("w", w_h, w), ("b", b_h, b),
        ("cot", cot_h, cot), ("srows_v", srows_h, srows_v), ("hrows_v", hrows_h, hrows_v),
    ]):
        loads[name] = pltpu.make_async_copy(src, dst, in_sem.at[i])
        loads[name].start()

    barrier = pltpu.get_barrier_semaphore()

    def zpeer(i):
        return xy * Z + lax.rem(z + i, Z)

    def xypeer(i):
        return lax.rem(xy + i, XY) * Z + z

    def signal(dev, core):
        pl.semaphore_signal(barrier, inc=1, device_id=(dev, core), device_id_type=MESH)

    def sig_z(i, c):
        signal(zpeer(i), g)
        signal(zpeer(i), 1 - g)
        return c

    def sig_xy(i, c):
        signal(xypeer(i), g)
        return c

    lax.fori_loop(1, Z, sig_z, 0)
    lax.fori_loop(1, XY, sig_xy, 0)
    signal(r, 1 - g)

    loads["feat"].wait()
    loads["srows"].wait()
    loads["hrows"].wait()

    def pack(i, c):
        slot = lax.rem(i, Z) * XY + i // Z
        for j in range(4):
            s1[slot, pl.ds(j, 1), :] = feat[pl.ds(srows[0, i * 4 + j], 1), :]
        return c

    lax.fori_loop(0, R, pack, 0, unroll=4)
    for j in range(4):
        hown[pl.ds(j, 1), :] = feat[pl.ds(hrows[0, j], 1), :]

    pl.semaphore_wait(barrier, 2 * (Z - 1) + (XY - 1) + 1)

    def remote(src, dst, k, dev, core):
        return pltpu.make_async_remote_copy(
            src_ref=src, dst_ref=dst, send_sem=ssem.at[k], recv_sem=rsem.at[k],
            device_id=(dev, core), device_id_type=MESH)

    def wait_recv(ref, k):
        pltpu.make_async_copy(ref, ref, rsem.at[k]).wait()

    def wait_send(ref, k):
        pltpu.make_async_copy(ref, ref, ssem.at[k]).wait()

    def send_hub_z(i, c):
        remote(hown, h1.at[z], 0, zpeer(i), g).start()
        return c

    def send_bnd_z(i, c):
        p = lax.rem(z + i, Z)
        remote(s1.at[pl.ds(p * XY, XY)], r1.at[z], 1, zpeer(i), g).start()
        return c

    lax.fori_loop(1, Z, send_hub_z, 0)
    pltpu.make_async_copy(hown, h1.at[z], rsem.at[0]).start()
    lax.fori_loop(1, Z, send_bnd_z, 0)
    pltpu.make_async_copy(s1.at[pl.ds(z * XY, XY)], r1.at[z], rsem.at[1]).start()

    loads["lcols"].wait()
    loads["lcount"].wait()
    loads["lv"].wait()
    lane = lax.broadcasted_iota(jnp.int32, (TB, 2 * TB), 1)
    upper = lane >= TB
    for t in range(N // TB):
        rows = pl.ds(t * TB, TB)
        dup = []
        for pair in range(KT // 2):
            v = lv[rows, pl.ds(pair * 2 * TB, 2 * TB)]
            turned = pltpu.roll(v, TB, 1)
            dup.append(jnp.where(upper, turned, v))
            dup.append(jnp.where(upper, v, turned))
        cols = [jnp.where(k < lcount[0, t], lcols[0, t * KT + k], -1) for k in range(KT)]
        for c in range(N // (2 * TB)):
            tile = jnp.where(upper, 2 * c + 1, 2 * c)
            out = jnp.zeros((TB, 2 * TB), F32)
            for k in range(KT):
                out = jnp.where(tile == cols[k], dup[k], out)
            high, low = split(out)
            ahi[rows, pl.ds(c * 2 * TB, 2 * TB)] = high
            alo[rows, pl.ds(c * 2 * TB, 2 * TB)] = low

    wait_recv(h1, 0)

    def send_hub_xy(i, c):
        remote(h1, hub.at[g, pl.ds(xy * Z, Z)], 2, xypeer(i), g).start()
        return c

    lax.fori_loop(1, XY, send_hub_xy, 0)
    pltpu.make_async_copy(h1, hub.at[g, pl.ds(xy * Z, Z)], rsem.at[2]).start()

    wait_recv(r1, 1)

    def send_bnd_xy(i, c):
        remote(r1.at[:, lax.rem(xy + i, XY)], br.at[pl.ds(xy * Z, Z)], 3, xypeer(i), g).start()
        return c

    lax.fori_loop(1, XY, send_bnd_xy, 0)
    pltpu.make_async_copy(r1.at[:, xy], br.at[pl.ds(xy * Z, Z)], rsem.at[3]).start()

    agg[...] = mm3(ahi[:, :N], alo[:, :N], wide(feat[...]))
    for c in range(N // 128):
        cols = pl.ds(c * 128, 128)
        athi[cols, :] = ahi[:, cols].astype(F32).T.astype(BF16)
        atlo[cols, :] = alo[:, cols].astype(F32).T.astype(BF16)

    loads["w"].wait()
    wv = w[...]
    wpair[...] = wide(wv)
    wt[...] = wide(wv.T)

    loads["bv"].wait()
    step = min(128, nb)
    for c in range(nb // step):
        v = bv[:, pl.ds(c * step, step)]
        high, low = split(v)
        ahi[:, pl.ds(N + c * step, step)] = high
        alo[:, pl.ds(N + c * step, step)] = low
        high, low = split(v.T)
        athi[pl.ds(N + c * step, step), :] = high
        atlo[pl.ds(N + c * step, step), :] = low

    loads["hv"].wait()
    step = min(128, nh)
    for c in range(nh // step):
        v = hv[:, pl.ds(c * step, step)]
        high, low = split(v)
        ahi[:, pl.ds(N + nb + c * step, step)] = high
        alo[:, pl.ds(N + nb + c * step, step)] = low
        high, low = split(v.T)
        for q in range(step // hb):
            block = c * (step // hb) + q
            to = N + nb + (block % 2) * (nh // 2) + (block // 2) * hb
            athi[pl.ds(to, hb), :] = high[q * hb:(q + 1) * hb]
            atlo[pl.ds(to, hb), :] = low[q * hb:(q + 1) * hb]

    wait_recv(hub.at[g], 2)
    to_sib = remote(hub.at[g], hub.at[g], 4, r, 1 - g)
    to_sib.start()
    wait_recv(br, 3)
    vb = br[...].reshape(nb, F)
    agg[...] += mm3(ahi[:, N:N + nb], alo[:, N:N + nb], wide(vb))
    to_sib.wait_recv()
    vh = jnp.concatenate([hub[0], hub[1]], axis=1).reshape(nh, F)
    agg[...] += mm3(ahi[:, N + nb:], alo[:, N + nb:], wide(vh))

    loads["b"].wait()
    loads["cot"].wait()
    H = w.shape[1]
    step = 128
    wsplit = wpair[...]
    for c in range(N // step):
        rows = pl.ds(c * step, step)
        high, low = split(agg[rows, :])
        both = mm(high, wsplit)
        v = both[:, :H] + both[:, H:] + mm(low, wsplit[:, :H]) + b[...]
        sq = v * v
        t = jnp.tanh(C0 * (v + C1 * (sq * v)))
        act_o[rows, :] = 0.5 * v * (1.0 + t)
        slope = 0.5 * (1.0 + t) + 0.5 * v * (1.0 - t * t) * (C0 * (1.0 + 3.0 * C1 * sq))
        prg[rows, :] = cot[rows, :] * slope
    high, low = split(prg[...])
    dag[...] = wide(mm3(high, low, wt[...]))

    g2 = dag[...]

    def back(start, size):
        return mm3(athi[pl.ds(start, size), :], atlo[pl.ds(start, size), :], g2)

    hbase = N + nb
    gs[...] = back(hbase + (1 - g) * (nh // 2), nh // 2)
    hub_sib = remote(gs, gsib, 5, r, 1 - g)
    hub_sib.start()
    bsend[...] = back(N, nb).reshape(R, 4, F)

    def bback_xy(i, c):
        p = lax.rem(xy + i, XY)
        remote(bsend.at[pl.ds(p * Z, Z)], bx.at[xy], 6, xypeer(i), g).start()
        return c

    lax.fori_loop(1, XY, bback_xy, 0)
    pltpu.make_async_copy(bsend.at[pl.ds(xy * Z, Z)], bx.at[xy], rsem.at[6]).start()

    own = back(hbase + g * (nh // 2), nh // 2)
    hub_sib.wait_recv()
    gown[...] = (own + gsib[...]).reshape(XY, hb, F)

    def hback_xy(i, c):
        remote(gown.at[lax.rem(xy + i, XY)], gx.at[xy], 7, xypeer(i), g).start()
        return c

    lax.fori_loop(1, XY, hback_xy, 0)
    pltpu.make_async_copy(gown.at[xy], gx.at[xy], rsem.at[7]).start()

    ag_t = agg[...].T
    ahigh, alow = split(ag_t)
    p2 = prg[...]
    wh, wl = split(p2)
    wterm = mm(ahigh, wh) + mm(ahigh, wl) + mm(alow, wh)
    piece = ws.shape[1]
    ws[...] = jnp.concatenate([wterm[:, :F], wterm[:, F:]], axis=0).reshape(XY, piece, F)

    def wxy(i, c):
        remote(ws.at[lax.rem(xy + i, XY)], wx.at[xy], 8, xypeer(i), g).start()
        return c

    lax.fori_loop(1, XY, wxy, 0)
    pltpu.make_async_copy(ws.at[xy], wx.at[xy], rsem.at[8]).start()

    fg_o[...] = back(0, N)

    wait_recv(bx, 6)

    def bback_z(i, c):
        p = lax.rem(z + i, Z)
        remote(bx.at[:, p], ar.at[z], 9, zpeer(i), g).start()
        return c

    lax.fori_loop(1, Z, bback_z, 0)
    pltpu.make_async_copy(bx.at[:, z], ar.at[z], rsem.at[9]).start()

    wait_recv(gx, 7)
    total = gx[0]
    for i in range(1, XY):
        total += gx[i]
    gp[...] = total.reshape(half, 8, F)

    for i in range(half):
        zi = half * g + i
        for core in range(2):
            mine = (zi == z) & (core == g)

            @pl.when(jnp.logical_not(mine))
            def _():
                remote(gp.at[i], gz.at[z], 10, xy * Z + zi, core).start()

            @pl.when(mine)
            def _():
                pltpu.make_async_copy(gp.at[i], gz.at[z], rsem.at[10]).start()

    wait_recv(wx, 8)
    total = wx[0]
    for i in range(1, XY):
        total += wx[i]
    wp[...] = total

    def wzs(i, c):
        remote(wp, wz.at[z], 11, zpeer(i), g).start()
        return c

    lax.fori_loop(1, Z, wzs, 0)
    pltpu.make_async_copy(wp, wz.at[z], rsem.at[11]).start()
    wait_recv(wz, 11)
    total = wz[0]
    for i in range(1, Z):
        total += wz[i]
    wsum[0] = total
    w_sib = remote(wsum.at[0], wsib, 12, r, 1 - g)
    w_sib.start()
    w_sib.wait_recv()
    wsum[1] = total + wsib[...]

    def wag(i, c):
        remote(wsum.at[1], wall.at[xy], 13, xypeer(i), g).start()
        return c

    lax.fori_loop(1, XY, wag, 0)
    pltpu.make_async_copy(wsum.at[1], wall.at[xy], rsem.at[13]).start()

    loads["srows_v"].wait()
    loads["hrows_v"].wait()
    node = lax.broadcasted_iota(jnp.int32, (N, nb), 0)
    pick = jnp.where(node == srows_v[...], 1.0, 0.0).astype(BF16)
    wait_recv(ar, 9)
    arr = jnp.concatenate([ar[i] for i in range(Z)], axis=1).reshape(nb, F)
    both = mm(pick, wide(arr))
    fg_o[...] += both[:, :F] + both[:, F:]

    wait_recv(gz, 10)
    total = gz[0]
    for i in range(1, Z):
        total += gz[i]
    node = lax.broadcasted_iota(jnp.int32, (N, F), 0)
    for j in range(4):
        row = jnp.where(g == 0, total[j:j + 1, :], total[4 + j:5 + j, :])
        fg_o[...] += jnp.where(node == hrows[0, j], row, 0.0)

    wait_recv(wall, 13)
    full = wall[...].reshape(2 * F, F) * float((R * 2 * N) ** -0.5)
    wg_o[:, :F] = full[:F]
    wg_o[:, F:] = full[F:]

    wait_send(h1.at[pl.ds(0, Z - 1)], 0)
    wait_send(s1.at[pl.ds(0, (Z - 1) * XY)], 1)
    wait_send(hub.at[0, pl.ds(0, (XY - 1) * Z)], 2)
    wait_send(br.at[pl.ds(0, (XY - 1) * Z)], 3)
    to_sib.wait_send()
    hub_sib.wait_send()
    wait_send(bsend.at[pl.ds(0, (XY - 1) * Z)], 6)
    wait_send(gown.at[pl.ds(0, XY - 1)], 7)
    wait_send(ws.at[pl.ds(0, XY - 1)], 8)
    wait_send(ar.at[pl.ds(0, Z - 1)], 9)

    @pl.when(z // half == g)
    def _():
        wait_send(gz.at[pl.ds(0, 2 * half - 1)], 10)

    @pl.when(z // half != g)
    def _():
        wait_send(gz.at[pl.ds(0, 2 * half)], 10)

    wait_send(wz.at[pl.ds(0, Z - 1)], 11)
    w_sib.wait_send()
    wait_send(wall.at[pl.ds(0, XY - 1)], 13)


def shards(features, weight, bias, cotangent, loc_vals, loc_cols, loc_count, hub_rows, hub_vals, send_rows, bnd_vals):
    rows = lax.axis_size("rows")
    Z = 8 if rows % 8 == 0 else 2
    XY = rows // Z
    N, F = features.shape
    H = weight.shape[1]
    nb = bnd_vals.shape[1]
    nh = hub_vals.shape[1]
    half = Z // 2
    hb = half * 8
    piece = 2 * F // XY
    K = N + nb + nh
    V = pltpu.VMEM
    D = pltpu.SemaphoreType.DMA
    any_ = pl.BlockSpec(memory_space=pl.ANY)
    vm = pl.BlockSpec(memory_space=pltpu.VMEM)
    scratch = [
        V((N, F), F32), V((F, H), F32), V((1, H), F32), V((N, H), F32), V((N, KT * TB), F32),
        pltpu.SMEM((1, N // TB * KT), jnp.int32), pltpu.SMEM((1, N // TB), jnp.int32),
        pltpu.SMEM((1, 4), jnp.int32), V((1, 4), jnp.int32),
        V((N, nh), F32), pltpu.SMEM((1, nb), jnp.int32), V((1, nb), jnp.int32), V((N, nb), F32),
        V((N, K), BF16), V((N, K), BF16), V((K, N), BF16), V((K, N), BF16),
        V((H, 2 * F), BF16), V((F, 2 * H), BF16),
        V((4, F), F32), V((rows, 4, F), F32), V((Z, XY, 4, F), F32), V((Z, 4, F), F32),
        V((rows, 4, F), F32), V((2, rows, 4, F), F32),
        V((N, F), F32), V((N, H), F32), V((N, 2 * F), BF16),
        V((nh // 2, F), F32), V((nh // 2, F), F32), V((XY, hb, F), F32), V((XY, hb, F), F32),
        V((half, 8, F), F32), V((Z, 8, F), F32),
        V((rows, 4, F), F32), V((XY, Z, 4, F), F32), V((Z, XY, 4, F), F32),
        V((XY, piece, F), F32), V((XY, piece, F), F32), V((piece, F), F32), V((Z, piece, F), F32),
        V((2, piece, F), F32), V((piece, F), F32), V((XY, piece, F), F32),
        D((13,)), D((1,)), D((14,)), D((14,)),
    ]
    return pl.pallas_call(
        functools.partial(kernel, XY, Z),
        out_shape=(
            jax.ShapeDtypeStruct((N, H), F32),
            jax.ShapeDtypeStruct((F, H), F32),
            jax.ShapeDtypeStruct((N, F), F32),
        ),
        in_specs=[any_] * 11,
        out_specs=(vm, vm, vm),
        scratch_shapes=scratch,
        compiler_params=pltpu.CompilerParams(
            collective_id=0, has_side_effects=True, vmem_limit_bytes=48 * 1024 * 1024
        ),
    )(
        features, weight, bias.reshape(1, H), cotangent, loc_vals, loc_cols.reshape(1, -1),
        loc_count.reshape(1, -1), hub_rows.reshape(1, 4), hub_vals,
        send_rows.reshape(1, nb), bnd_vals,
    )


def solution(mesh):
    node = P(("rows", "grp"), None)
    flat = P(("rows", "grp"))
    return jax.shard_map(
        shards,
        mesh=mesh,
        in_specs=(node, P(), P(), node, node, node, flat, flat, node, P(("rows", "grp"), None, None), node),
        out_specs=(node, P(), node),
        check_vma=False,
    )
```

```python
import functools
import math

import jax
import jax.numpy as jnp
from jax import lax
from jax.experimental import pallas as pl
from jax.experimental.pallas import tpu as pltpu
from jax.sharding import PartitionSpec as P

TB = 64
KT = 4
MESH = pl.DeviceIdType.MESH
F32 = jnp.float32
BF16 = jnp.bfloat16
C0 = math.sqrt(2.0 / math.pi)
C1 = 0.044715


def split(value):
    high = value.astype(BF16)
    low = (value - high.astype(F32)).astype(BF16)
    return high, low


def mm(left, right):
    return jnp.dot(left, right, preferred_element_type=F32)


def wide(value):
    high, low = split(value)
    return jnp.concatenate([high, low], axis=1)


def mm3(high, low, pair):
    n = pair.shape[1] // 2
    both = mm(high, pair)
    return both[:, :n] + both[:, n:] + mm(low, pair[:, :n])


def kernel(
    X, Y, Z,
    feat_h, w_h, b_h, cot_h, lv_h, lcols_h, lcount_h, hrows_h, hv_h, srows_h, bv_h,
    act_o, wg_o, fg_o,
    feat, w, b, cot, lv, lcols, lcount, hrows, hv, srows, srows_v, bv,
    ahi, alo, athi, atlo, wt, wpair,
    hown, s1, h1, br, hub,
    agg, prg, dag,
    gs, gsib, gown, gx, gp, gz,
    bsend, ar,
    ws, wx, wp, wz, wsum, wall,
    in_sem, ssem, rsem, plane_sem,
):
    r = lax.axis_index("rows")
    g = lax.axis_index("grp")
    xy = r // Z
    z = lax.rem(r, Z)
    half = Z // 2
    XY = X * Y
    R = XY * Z
    F = feat.shape[1]
    N = feat.shape[0]
    nb = bv.shape[1]
    nh = hv.shape[1]
    hb = half * 8

    loads = {}

    def load(*names):
        for name in names:
            src, dst, i = arrays[name]
            loads[name] = pltpu.make_async_copy(src, dst, in_sem.at[i])
            loads[name].start()

    arrays = {}
    for i, (name, src, dst) in enumerate([
        ("feat", feat_h, feat), ("srows", srows_h, srows), ("hrows", hrows_h, hrows),
        ("lcols", lcols_h, lcols), ("lcount", lcount_h, lcount),
        ("lv", lv_h, lv), ("bv", bv_h, bv), ("hv", hv_h, hv), ("w", w_h, w), ("b", b_h, b),
        ("cot", cot_h, cot), ("srows_v", srows_h, srows_v),
    ]):
        arrays[name] = (src, dst, i)
    load("srows", "hrows", "feat")

    barrier = pltpu.get_barrier_semaphore()
    x = xy // Y
    y = lax.rem(xy, Y)
    z_order = sorted(range(1, Z), key=lambda d: -min(d, Z - d))
    xy_order = sorted(
        ((dx, dy) for dx in range(X) for dy in range(Y)),
        key=lambda d: -min(d[0], X - d[0]) - min(d[1], Y - d[1]))[:-1]

    def zline(d):
        return lax.rem(z + d, Z)

    def plane(d):
        return lax.rem(x + d[0], X) * Y + lax.rem(y + d[1], Y)

    def signal(sem, dev, core):
        pl.semaphore_signal(sem, inc=1, device_id=(dev, core), device_id_type=MESH)

    for d in z_order:
        signal(barrier, xy * Z + zline(d), g)
    for d in xy_order:
        signal(barrier, plane(d) * Z + z, g)
    for d in z_order:
        signal(barrier, xy * Z + zline(d), 1 - g)
    for d in xy_order:
        signal(barrier, plane(d) * Z + z, 1 - g)
    signal(barrier, r, 1 - g)
    load("lcols", "lcount", "lv", "w", "b", "srows_v")

    loads["srows"].wait()
    loads["hrows"].wait()
    loads["feat"].wait()

    def pack(i, c):
        for j in range(4):
            s1[i, pl.ds(j, 1), :] = feat[pl.ds(srows[j, i], 1), :]
        return c

    for j in range(4):
        hown[pl.ds(j, 1), :] = feat[pl.ds(hrows[0, j], 1), :]
    lax.fori_loop(0, R, pack, 0, unroll=4)
    load("bv", "hv", "cot")

    pl.semaphore_wait(barrier, 2 * (Z - 1) + 2 * (XY - 1) + 1)

    for d in z_order:
        signal(plane_sem, xy * Z + zline(d), g)

    def remote(src, dst, k, dev, core):
        return pltpu.make_async_remote_copy(
            src_ref=src, dst_ref=dst, send_sem=ssem.at[k], recv_sem=rsem.at[k],
            device_id=(dev, core), device_id_type=MESH)

    def wait_recv(ref, k):
        pltpu.make_async_copy(ref, ref, rsem.at[k]).wait()

    def wait_send(ref, k):
        pltpu.make_async_copy(ref, ref, ssem.at[k]).wait()

    def each(order, send):
        def step(d, k, c):
            back = (k + 1) // 2
            dz = lax.rem(Z // 2 + lax.rem(k, 2) * (Z - 2 * back) + back, Z)
            send(plane(d) * Z + zline(dz))
            return c

        for d in order:
            lax.fori_loop(0, Z, functools.partial(step, d), 0)

    def rest(send):
        for d in z_order:
            send(xy * Z + zline(d))

    first, second = xy_order[:len(xy_order) // 2], xy_order[len(xy_order) // 2:]

    def send_bnd(p):
        remote(s1.at[p], br.at[r], 3, p, g).start()

    for d in z_order:
        remote(hown, h1.at[z], 0, xy * Z + zline(d), g).start()
    pltpu.make_async_copy(hown, h1.at[z], rsem.at[0]).start()
    pltpu.make_async_copy(s1.at[r], br.at[r], rsem.at[3]).start()
    wait_recv(h1, 0)
    for d in xy_order:
        remote(h1, hub.at[g, pl.ds(xy * Z, Z)], 2, plane(d) * Z + z, g).start()
    pltpu.make_async_copy(h1, hub.at[g, pl.ds(xy * Z, Z)], rsem.at[2]).start()
    pl.semaphore_wait(plane_sem, Z - 1)
    each(first + second, send_bnd)
    rest(send_bnd)

    loads["lcols"].wait()
    loads["lcount"].wait()
    loads["lv"].wait()
    lane = lax.broadcasted_iota(jnp.int32, (TB, 2 * TB), 1)
    upper = lane >= TB
    for t in range(N // TB):
        rows = pl.ds(t * TB, TB)
        dup = []
        for pair in range(KT // 2):
            v = lv[rows, pl.ds(pair * 2 * TB, 2 * TB)]
            turned = pltpu.roll(v, TB, 1)
            dup.append(jnp.where(upper, turned, v))
            dup.append(jnp.where(upper, v, turned))
        cols = [jnp.where(k < lcount[0, t], lcols[k, t], -1) for k in range(KT)]
        for c in range(N // (2 * TB)):
            tile = jnp.where(upper, 2 * c + 1, 2 * c)
            out = jnp.zeros((TB, 2 * TB), F32)
            for k in range(KT):
                out = jnp.where(tile == cols[k], dup[k], out)
            high, low = split(out)
            ahi[rows, pl.ds(c * 2 * TB, 2 * TB)] = high
            alo[rows, pl.ds(c * 2 * TB, 2 * TB)] = low

    agg[...] = mm3(ahi[:, :N], alo[:, :N], wide(feat[...]))
    for c in range(N // 128):
        cols = pl.ds(c * 128, 128)
        athi[cols, :] = ahi[:, cols].astype(F32).T.astype(BF16)
        atlo[cols, :] = alo[:, cols].astype(F32).T.astype(BF16)

    loads["w"].wait()
    wv = w[...]
    wpair[...] = wide(wv)
    wt[...] = wide(wv.T)

    loads["bv"].wait()
    step = min(128, nb)
    for c in range(nb // step):
        v = bv[:, pl.ds(c * step, step)]
        high, low = split(v)
        ahi[:, pl.ds(N + c * step, step)] = high
        alo[:, pl.ds(N + c * step, step)] = low
        high, low = split(v.T)
        athi[pl.ds(N + c * step, step), :] = high
        atlo[pl.ds(N + c * step, step), :] = low

    loads["hv"].wait()
    step = min(128, nh)
    for c in range(nh // step):
        v = hv[:, pl.ds(c * step, step)]
        high, low = split(v)
        ahi[:, pl.ds(N + nb + c * step, step)] = high
        alo[:, pl.ds(N + nb + c * step, step)] = low
        high, low = split(v.T)
        for q in range(step // hb):
            block = c * (step // hb) + q
            to = N + nb + (block % 2) * (nh // 2) + (block // 2) * hb
            athi[pl.ds(to, hb), :] = high[q * hb:(q + 1) * hb]
            atlo[pl.ds(to, hb), :] = low[q * hb:(q + 1) * hb]

    wait_recv(hub.at[g], 2)
    to_sib = remote(hub.at[g], hub.at[g], 4, r, 1 - g)
    to_sib.start()
    wait_recv(br, 3)
    vb = br[...].reshape(nb, F)
    agg[...] += mm3(ahi[:, N:N + nb], alo[:, N:N + nb], wide(vb))
    to_sib.wait_recv()
    vh = jnp.concatenate([hub[0], hub[1]], axis=1).reshape(nh, F)
    agg[...] += mm3(ahi[:, N + nb:], alo[:, N + nb:], wide(vh))

    loads["b"].wait()
    loads["cot"].wait()
    H = w.shape[1]
    step = 128
    wsplit = wpair[...]
    for c in range(N // step):
        rows = pl.ds(c * step, step)
        high, low = split(agg[rows, :])
        both = mm(high, wsplit)
        v = both[:, :H] + both[:, H:] + mm(low, wsplit[:, :H]) + b[...]
        sq = v * v
        t = jnp.tanh(C0 * (v + C1 * (sq * v)))
        act_o[rows, :] = 0.5 * v * (1.0 + t)
        slope = 0.5 * (1.0 + t) + 0.5 * v * (1.0 - t * t) * (C0 * (1.0 + 3.0 * C1 * sq))
        prg[rows, :] = cot[rows, :] * slope
    ahigh, alow = split(agg[...].T)
    wh, wl = split(prg[...])
    wterm = mm(ahigh, wh) + mm(ahigh, wl) + mm(alow, wh)
    piece = ws.shape[2]
    ws[...] = jnp.concatenate([wterm[:, :F], wterm[:, F:]], axis=0).reshape(XY, 2, piece, F)

    for d in xy_order:
        for core in (g, 1 - g):
            remote(ws.at[plane(d), core], wx.at[xy * 2 + g], 8, plane(d) * Z + z, core).start()
    remote(ws.at[xy, 1 - g], wx.at[xy * 2 + g], 8, r, 1 - g).start()
    pltpu.make_async_copy(ws.at[xy, g], wx.at[xy * 2 + g], rsem.at[8]).start()

    high, low = split(prg[...])
    dag[...] = wide(mm3(high, low, wt[...]))

    g2 = dag[...]

    def back(start, size):
        return mm3(athi[pl.ds(start, size), :], atlo[pl.ds(start, size), :], g2)

    hbase = N + nb
    gs[...] = back(hbase + (1 - g) * (nh // 2), nh // 2)
    hub_sib = remote(gs, gsib, 5, r, 1 - g)
    hub_sib.start()
    bsend[...] = back(N, nb).reshape(R, 4, F)

    def send_back(p):
        remote(bsend.at[p], ar.at[r], 6, p, g).start()

    pltpu.make_async_copy(bsend.at[r], ar.at[r], rsem.at[6]).start()
    each(first, send_back)

    own = back(hbase + g * (nh // 2), nh // 2)
    hub_sib.wait_recv()
    gown[...] = (own + gsib[...]).reshape(XY, hb, F)
    for d in xy_order:
        remote(gown.at[plane(d)], gx.at[xy], 7, plane(d) * Z + z, g).start()
    pltpu.make_async_copy(gown.at[xy], gx.at[xy], rsem.at[7]).start()

    wait_recv(wx, 8)
    total = wx[0]
    for i in range(1, 2 * XY):
        total += wx[i]
    wp[...] = total
    for d in z_order:
        remote(wp, wz.at[z], 11, xy * Z + zline(d), g).start()
    pltpu.make_async_copy(wp, wz.at[z], rsem.at[11]).start()

    each(second, send_back)
    rest(send_back)

    wait_recv(gx, 7)
    total = gx[0]
    for i in range(1, XY):
        total += gx[i]
    gp[...] = total.reshape(half, 8, F)

    for i in range(half):
        zi = half * g + i
        for core in range(2):
            mine = (zi == z) & (core == g)

            @pl.when(jnp.logical_not(mine))
            def _():
                remote(gp.at[i], gz.at[z], 10, xy * Z + zi, core).start()

            @pl.when(mine)
            def _():
                pltpu.make_async_copy(gp.at[i], gz.at[z], rsem.at[10]).start()

    fg_o[...] = back(0, N)

    wait_recv(wz, 11)
    total = wz[0]
    for i in range(1, Z):
        total += wz[i]
    wsum[...] = total

    for d in xy_order:
        for core in (g, 1 - g):
            remote(wsum, wall.at[xy * 2 + g], 13, plane(d) * Z + z, core).start()
    remote(wsum, wall.at[xy * 2 + g], 13, r, 1 - g).start()
    pltpu.make_async_copy(wsum, wall.at[xy * 2 + g], rsem.at[13]).start()

    loads["srows_v"].wait()
    node = lax.broadcasted_iota(jnp.int32, (N, R), 0)
    picks = [jnp.where(node == srows_v[pl.ds(j, 1), :], 1.0, 0.0).astype(BF16) for j in range(4)]
    pick = jnp.concatenate(picks, axis=1)
    wait_recv(ar, 6)
    arr = jnp.concatenate([ar[:, j, :] for j in range(4)], axis=0)
    both = mm(pick, wide(arr))
    fg_o[...] += both[:, :F] + both[:, F:]

    wait_recv(gz, 10)
    total = gz[0]
    for i in range(1, Z):
        total += gz[i]
    node = lax.broadcasted_iota(jnp.int32, (N, F), 0)
    for j in range(4):
        row = jnp.where(g == 0, total[j:j + 1, :], total[4 + j:5 + j, :])
        fg_o[...] += jnp.where(node == hrows[0, j], row, 0.0)

    wait_recv(wall, 13)
    full = wall[...].reshape(2 * F, F) * float((R * 2 * N) ** -0.5)
    wg_o[:, :F] = full[:F]
    wg_o[:, F:] = full[F:]

    wait_send(h1.at[pl.ds(0, Z - 1)], 0)
    wait_send(hub.at[0, pl.ds(0, (XY - 1) * Z)], 2)
    wait_send(br.at[pl.ds(0, R - 1)], 3)
    to_sib.wait_send()
    hub_sib.wait_send()
    wait_send(ar.at[pl.ds(0, R - 1)], 6)
    wait_send(gown.at[pl.ds(0, XY - 1)], 7)
    wait_send(wx.at[pl.ds(0, 2 * XY - 1)], 8)

    @pl.when(z // half == g)
    def _():
        wait_send(gz.at[pl.ds(0, 2 * half - 1)], 10)

    @pl.when(z // half != g)
    def _():
        wait_send(gz.at[pl.ds(0, 2 * half)], 10)

    wait_send(wz.at[pl.ds(0, Z - 1)], 11)
    wait_send(wall.at[pl.ds(0, 2 * XY - 1)], 13)


def write_out(a_ref, b_ref, c_ref, a_out, b_out, c_out, sems):
    copies = [
        pltpu.make_async_copy(a_ref, a_out, sems.at[0]),
        pltpu.make_async_copy(b_ref, b_out, sems.at[1]),
        pltpu.make_async_copy(c_ref, c_out, sems.at[2]),
    ]
    for copy in copies:
        copy.start()
    for copy in copies:
        copy.wait()


def shards(features, weight, bias, cotangent, loc_vals, loc_cols, loc_count, hub_rows, hub_vals, send_rows, bnd_vals):
    rows = lax.axis_size("rows")
    Z = 8 if rows % 8 == 0 else 2
    XY = rows // Z
    Y = 4 if XY % 4 == 0 else 1
    X = XY // Y
    N, F = features.shape
    H = weight.shape[1]
    nb = bnd_vals.shape[1]
    nh = hub_vals.shape[1]
    half = Z // 2
    hb = half * 8
    piece = F // XY
    K = N + nb + nh
    V = pltpu.VMEM
    D = pltpu.SemaphoreType.DMA
    hbm = pl.BlockSpec(memory_space=pltpu.HBM)
    vm = pl.BlockSpec(memory_space=pltpu.VMEM)
    scratch = [
        V((N, F), F32), V((F, H), F32), V((1, H), F32), V((N, H), F32), V((N, KT * TB), F32),
        pltpu.SMEM((KT, N // TB), jnp.int32), pltpu.SMEM((1, N // TB), jnp.int32),
        pltpu.SMEM((1, 4), jnp.int32),
        V((N, nh), F32), pltpu.SMEM((4, rows), jnp.int32), V((4, rows), jnp.int32), V((N, nb), F32),
        V((N, K), BF16), V((N, K), BF16), V((K, N), BF16), V((K, N), BF16),
        V((H, 2 * F), BF16), V((F, 2 * H), BF16),
        V((4, F), F32), V((rows, 4, F), F32), V((Z, 4, F), F32),
        V((rows, 4, F), F32), V((2, rows, 4, F), F32),
        V((N, F), F32), V((N, H), F32), V((N, 2 * F), BF16),
        V((nh // 2, F), F32), V((nh // 2, F), F32), V((XY, hb, F), F32), V((XY, hb, F), F32),
        V((half, 8, F), F32), V((Z, 8, F), F32),
        V((rows, 4, F), F32), V((rows, 4, F), F32),
        V((XY, 2, piece, F), F32), V((2 * XY, piece, F), F32), V((piece, F), F32), V((Z, piece, F), F32),
        V((piece, F), F32), V((2 * XY, piece, F), F32),
        D((12,)), D((14,)), D((14,)), pltpu.SemaphoreType.REGULAR,
    ]
    results = pl.pallas_call(
        functools.partial(kernel, X, Y, Z),
        out_shape=(pltpu.VMEM((N, H), F32), pltpu.VMEM((F, H), F32), pltpu.VMEM((N, F), F32)),
        in_specs=[hbm] * 11,
        out_specs=(vm, vm, vm),
        scratch_shapes=scratch,
        compiler_params=pltpu.CompilerParams(
            collective_id=0, has_side_effects=True, vmem_limit_bytes=60 * 1024 * 1024
        ),
    )(
        features, weight, bias.reshape(1, H), cotangent, loc_vals, loc_cols.T,
        loc_count.reshape(1, -1), hub_rows.reshape(1, 4), hub_vals,
        send_rows[0].T, bnd_vals,
    )
    return pl.pallas_call(
        write_out,
        out_shape=(
            jax.ShapeDtypeStruct((N, H), F32),
            jax.ShapeDtypeStruct((F, H), F32),
            jax.ShapeDtypeStruct((N, F), F32),
        ),
        in_specs=[vm] * 3,
        out_specs=(pl.BlockSpec(memory_space=pl.ANY),) * 3,
        scratch_shapes=[D((3,))],
        compiler_params=pltpu.CompilerParams(vmem_limit_bytes=4 * 1024 * 1024),
    )(*results)


def solution(mesh):
    node = P(("rows", "grp"), None)
    flat = P(("rows", "grp"))
    return jax.shard_map(
        shards,
        mesh=mesh,
        in_specs=(node, P(), P(), node, node, node, flat, flat, node, P(("rows", "grp"), None, None), node),
        out_specs=(node, P(), node),
        check_vma=False,
    )
```

```python
import functools
import math

import jax
import jax.numpy as jnp
from jax import lax
from jax.experimental import pallas as pl
from jax.experimental.pallas import tpu as pltpu
from jax.sharding import PartitionSpec as P

TB = 64
KT = 4
MESH = pl.DeviceIdType.MESH
F32 = jnp.float32
BF16 = jnp.bfloat16
C0 = math.sqrt(2.0 / math.pi)
C1 = 0.044715


def split(value):
    high = value.astype(BF16)
    low = (value - high.astype(F32)).astype(BF16)
    return high, low


def mm(left, right):
    return jnp.dot(left, right, preferred_element_type=F32)


def wide(value):
    high, low = split(value)
    return jnp.concatenate([high, low], axis=1)


def mm3(high, low, pair):
    n = pair.shape[1] // 2
    both = mm(high, pair)
    return both[:, :n] + both[:, n:] + mm(low, pair[:, :n])


def kernel(
    X, Y, Z,
    feat_h, w_h, b_h, cot_h, lv_h, lcols_h, lcount_h, hrows_h, hv_h, srows_h, bv_h,
    act_o, wg_o, fg_o,
    feat, w, b, cot, lv, lcols, lcount, hrows, hv, srows, srows_v, bv,
    ahi, alo, athi, atlo, wt, wpair,
    hown, s1, h1, br, hub,
    agg, prg, dag,
    gs, gsib, gown, gx, gp, gz,
    bsend, ar,
    ws, wx, wp, wsib, wz, wsum, wall,
    in_sem, ssem, rsem, plane_sem,
):
    r = lax.axis_index("rows")
    g = lax.axis_index("grp")
    xy = r // Z
    z = lax.rem(r, Z)
    XY = X * Y
    R = XY * Z
    F = feat.shape[1]
    N = feat.shape[0]
    nb = bv.shape[1]
    nh = hv.shape[1]
    hb = Z * 4

    loads = {}

    def load(*names):
        for name in names:
            src, dst, i = arrays[name]
            loads[name] = pltpu.make_async_copy(src, dst, in_sem.at[i])
            loads[name].start()

    arrays = {}
    for i, (name, src, dst) in enumerate([
        ("feat", feat_h, feat), ("srows", srows_h, srows), ("hrows", hrows_h, hrows),
        ("lcols", lcols_h, lcols), ("lcount", lcount_h, lcount),
        ("lv", lv_h, lv), ("bv", bv_h, bv), ("hv", hv_h, hv), ("w", w_h, w), ("b", b_h, b),
        ("cot", cot_h, cot), ("srows_v", srows_h, srows_v),
    ]):
        arrays[name] = (src, dst, i)
    load("srows", "hrows", "feat")

    barrier = pltpu.get_barrier_semaphore()
    x = xy // Y
    y = lax.rem(xy, Y)
    z_order = sorted(range(1, Z), key=lambda d: -min(d, Z - d))
    xy_order = sorted(
        ((dx, dy) for dx in range(X) for dy in range(Y)),
        key=lambda d: -min(d[0], X - d[0]) - min(d[1], Y - d[1]))[:-1]

    def zline(d):
        return lax.rem(z + d, Z)

    def plane(d):
        return lax.rem(x + d[0], X) * Y + lax.rem(y + d[1], Y)

    def signal(sem, dev, core):
        pl.semaphore_signal(sem, inc=1, device_id=(dev, core), device_id_type=MESH)

    for d in z_order:
        signal(barrier, xy * Z + zline(d), g)
    for d in xy_order:
        signal(barrier, plane(d) * Z + z, g)
    signal(barrier, r, 1 - g)
    load("lcols", "lcount", "lv", "w", "b", "srows_v")

    loads["hrows"].wait()
    loads["feat"].wait()
    for j in range(4):
        hown[pl.ds(j, 1), :] = feat[pl.ds(hrows[0, j], 1), :]

    pl.semaphore_wait(barrier, (Z - 1) + (XY - 1) + 1)

    for d in z_order:
        signal(plane_sem.at[z], xy * Z + zline(d), g)

    def remote(src, dst, k, dev, core):
        return pltpu.make_async_remote_copy(
            src_ref=src, dst_ref=dst, send_sem=ssem.at[k], recv_sem=rsem.at[k],
            device_id=(dev, core), device_id_type=MESH)

    def wait_recv(ref, k):
        pltpu.make_async_copy(ref, ref, rsem.at[k]).wait()

    def wait_send(ref, k):
        pltpu.make_async_copy(ref, ref, ssem.at[k]).wait()

    def each(order, send):
        def step(d, k, c):
            back = (k + 1) // 2
            dz = lax.rem(Z // 2 + lax.rem(k, 2) * (Z - 2 * back) + back, Z)
            send(plane(d) * Z + zline(dz))
            return c

        for d in order:
            lax.fori_loop(0, Z, functools.partial(step, d), 0)

    def rest(send):
        for d in z_order:
            send(xy * Z + zline(d))

    first, second = xy_order[:len(xy_order) // 2], xy_order[len(xy_order) // 2:]

    def send_bnd(p):
        remote(s1.at[p], br.at[r], 3, p, g).start()

    for d in z_order:
        remote(hown, h1.at[z], 0, xy * Z + zline(d), g).start()
    pltpu.make_async_copy(hown, h1.at[z], rsem.at[0]).start()

    loads["srows"].wait()

    def pack(i, c):
        for j in range(4):
            s1[i, pl.ds(j, 1), :] = feat[pl.ds(srows[j, i], 1), :]
        return c

    lax.fori_loop(0, R, pack, 0, unroll=4)
    load("bv", "hv", "cot")
    pltpu.make_async_copy(s1.at[r], br.at[r], rsem.at[3]).start()
    for d in xy_order:
        send_bnd(plane(d) * Z + z)

    for pair in range(1, Z // 2 + 1):
        for d in sorted({pair, Z - pair}):
            pl.semaphore_wait(plane_sem.at[zline(d)], 1)
        for dxy in xy_order + [(0, 0)]:
            for d in sorted({pair, Z - pair}):
                send_bnd(plane(dxy) * Z + zline(d))
    wait_recv(h1, 0)
    for d in xy_order:
        remote(h1, hub.at[g, pl.ds(xy * Z, Z)], 2, plane(d) * Z + z, g).start()
    pltpu.make_async_copy(h1, hub.at[g, pl.ds(xy * Z, Z)], rsem.at[2]).start()

    loads["lcols"].wait()
    loads["lcount"].wait()
    loads["lv"].wait()
    lane = lax.broadcasted_iota(jnp.int32, (TB, 2 * TB), 1)
    upper = lane >= TB
    for t in range(N // TB):
        rows = pl.ds(t * TB, TB)
        dup = []
        for pair in range(KT // 2):
            v = lv[rows, pl.ds(pair * 2 * TB, 2 * TB)]
            turned = pltpu.roll(v, TB, 1)
            dup.append(jnp.where(upper, turned, v))
            dup.append(jnp.where(upper, v, turned))
        cols = [jnp.where(k < lcount[0, t], lcols[k, t], -1) for k in range(KT)]
        for c in range(N // (2 * TB)):
            tile = jnp.where(upper, 2 * c + 1, 2 * c)
            out = jnp.zeros((TB, 2 * TB), F32)
            for k in range(KT):
                out = jnp.where(tile == cols[k], dup[k], out)
            high, low = split(out)
            ahi[rows, pl.ds(c * 2 * TB, 2 * TB)] = high
            alo[rows, pl.ds(c * 2 * TB, 2 * TB)] = low

    agg[...] = mm3(ahi[:, :N], alo[:, :N], wide(feat[...]))
    for c in range(N // 128):
        cols = pl.ds(c * 128, 128)
        athi[cols, :] = ahi[:, cols].astype(F32).T.astype(BF16)
        atlo[cols, :] = alo[:, cols].astype(F32).T.astype(BF16)

    loads["w"].wait()
    wv = w[...]
    wpair[...] = wide(wv)
    wt[...] = wide(wv.T)

    loads["bv"].wait()
    step = min(128, nb)
    for c in range(nb // step):
        v = bv[:, pl.ds(c * step, step)]
        high, low = split(v)
        ahi[:, pl.ds(N + c * step, step)] = high
        alo[:, pl.ds(N + c * step, step)] = low
        high, low = split(v.T)
        athi[pl.ds(N + c * step, step), :] = high
        atlo[pl.ds(N + c * step, step), :] = low

    loads["hv"].wait()
    step = min(128, nh)
    for c in range(nh // step):
        v = hv[:, pl.ds(c * step, step)]
        high, low = split(v)
        ahi[:, pl.ds(N + nb + c * step, step)] = high
        alo[:, pl.ds(N + nb + c * step, step)] = low
        turned = v.T.reshape(step // 8, 8, N)
        for core in range(2):
            high, low = split(turned[:, core * 4:core * 4 + 4, :].reshape(step // 2, N))
            to = pl.ds(N + nb + core * (nh // 2) + c * (step // 2), step // 2)
            athi[to, :] = high
            atlo[to, :] = low

    wait_recv(hub.at[g], 2)
    to_sib = remote(hub.at[g], hub.at[g], 4, r, 1 - g)
    to_sib.start()
    to_sib.wait_recv()
    vh = jnp.concatenate([hub[0], hub[1]], axis=1).reshape(nh, F)
    agg[...] += mm3(ahi[:, N + nb:], alo[:, N + nb:], wide(vh))
    wait_recv(br, 3)
    vb = br[...].reshape(nb, F)
    agg[...] += mm3(ahi[:, N:N + nb], alo[:, N:N + nb], wide(vb))

    loads["b"].wait()
    loads["cot"].wait()
    H = w.shape[1]
    step = 128
    wsplit = wpair[...]
    for c in range(N // step):
        rows = pl.ds(c * step, step)
        high, low = split(agg[rows, :])
        both = mm(high, wsplit)
        v = both[:, :H] + both[:, H:] + mm(low, wsplit[:, :H]) + b[...]
        sq = v * v
        t = jnp.tanh(C0 * (v + C1 * (sq * v)))
        act_o[rows, :] = 0.5 * v * (1.0 + t)
        slope = 0.5 * (1.0 + t) + 0.5 * v * (1.0 - t * t) * (C0 * (1.0 + 3.0 * C1 * sq))
        prg[rows, :] = cot[rows, :] * slope
    ahigh, alow = split(agg[...].T)
    wh, wl = split(prg[...])
    wterm = mm(ahigh, wh) + mm(ahigh, wl) + mm(alow, wh)
    ws[...] = jnp.concatenate([wterm[:, :F], wterm[:, F:]], axis=0).reshape(ws.shape)
    for d in xy_order:
        remote(ws.at[plane(d)], wx.at[xy], 8, plane(d) * Z + z, g).start()
    pltpu.make_async_copy(ws.at[xy], wx.at[xy], rsem.at[8]).start()

    high, low = split(prg[...])
    dag[...] = wide(mm3(high, low, wt[...]))

    g2 = dag[...]

    def back(start, size):
        return mm3(athi[pl.ds(start, size), :], atlo[pl.ds(start, size), :], g2)

    hbase = N + nb
    gs[...] = back(hbase + (1 - g) * (nh // 2), nh // 2)
    hub_sib = remote(gs, gsib, 5, r, 1 - g)
    hub_sib.start()
    own = back(hbase + g * (nh // 2), nh // 2)
    bsend[...] = back(N, nb).reshape(R, 4, F)
    hub_sib.wait_recv()
    gown[...] = (own + gsib[...]).reshape(XY, hb, F)
    for d in xy_order:
        remote(gown.at[plane(d)], gx.at[xy], 7, plane(d) * Z + z, g).start()
    pltpu.make_async_copy(gown.at[xy], gx.at[xy], rsem.at[7]).start()

    def send_back(p):
        remote(bsend.at[p], ar.at[r], 6, p, g).start()

    pltpu.make_async_copy(bsend.at[r], ar.at[r], rsem.at[6]).start()
    each(first, send_back)

    wait_recv(wx, 8)
    total = wx[0]
    for i in range(1, XY):
        total += wx[i]
    wp[0] = total
    w_sib = remote(wp.at[0], wsib, 12, r, 1 - g)
    w_sib.start()
    w_sib.wait_recv()
    wp[1] = total + wsib[...]
    for d in z_order:
        remote(wp.at[1], wz.at[z], 11, xy * Z + zline(d), g).start()
    pltpu.make_async_copy(wp.at[1], wz.at[z], rsem.at[11]).start()

    each(second, send_back)
    rest(send_back)

    fg_o[...] = back(0, N)

    wait_recv(gx, 7)
    total = gx[0]
    for i in range(1, XY):
        total += gx[i]
    gp[...] = total.reshape(Z, 4, F)
    for d in z_order:
        remote(gp.at[zline(d)], gz.at[z], 10, xy * Z + zline(d), g).start()
    pltpu.make_async_copy(gp.at[z], gz.at[z], rsem.at[10]).start()

    wait_recv(wz, 11)
    total = wz[0]
    for i in range(1, Z):
        total += wz[i]
    wsum[...] = total

    for d in xy_order:
        remote(wsum, wall.at[xy], 13, plane(d) * Z + z, g).start()
    pltpu.make_async_copy(wsum, wall.at[xy], rsem.at[13]).start()

    loads["srows_v"].wait()
    node = lax.broadcasted_iota(jnp.int32, (N, R), 0)
    picks = [jnp.where(node == srows_v[pl.ds(j, 1), :], 1.0, 0.0).astype(BF16) for j in range(4)]
    pick = jnp.concatenate(picks, axis=1)
    wait_recv(ar, 6)
    arr = jnp.concatenate([ar[:, j, :] for j in range(4)], axis=0)
    both = mm(pick, wide(arr))
    fg_o[...] += both[:, :F] + both[:, F:]

    wait_recv(gz, 10)
    total = gz[0]
    for i in range(1, Z):
        total += gz[i]
    node = lax.broadcasted_iota(jnp.int32, (N, F), 0)
    for j in range(4):
        fg_o[...] += jnp.where(node == hrows[0, j], total[j:j + 1, :], 0.0)

    wait_recv(wall, 13)
    full = wall[...].reshape(2 * F, F) * float((R * 2 * N) ** -0.5)
    wg_o[:, :F] = full[:F]
    wg_o[:, F:] = full[F:]

    wait_send(h1.at[pl.ds(0, Z - 1)], 0)
    wait_send(hub.at[0, pl.ds(0, (XY - 1) * Z)], 2)
    wait_send(br.at[pl.ds(0, R - 1)], 3)
    to_sib.wait_send()
    hub_sib.wait_send()
    wait_send(ar.at[pl.ds(0, R - 1)], 6)
    wait_send(gown.at[pl.ds(0, XY - 1)], 7)
    wait_send(wx.at[pl.ds(0, XY - 1)], 8)

    wait_send(gz.at[pl.ds(0, Z - 1)], 10)
    wait_send(wz.at[pl.ds(0, Z - 1)], 11)
    w_sib.wait_send()
    wait_send(wall.at[pl.ds(0, XY - 1)], 13)


def write_out(a_ref, b_ref, c_ref, a_out, b_out, c_out, sems):
    copies = [
        pltpu.make_async_copy(a_ref, a_out, sems.at[0]),
        pltpu.make_async_copy(b_ref, b_out, sems.at[1]),
        pltpu.make_async_copy(c_ref, c_out, sems.at[2]),
    ]
    for copy in copies:
        copy.start()
    for copy in copies:
        copy.wait()


def shards(features, weight, bias, cotangent, loc_vals, loc_cols, loc_count, hub_rows, hub_vals, send_rows, bnd_vals):
    rows = lax.axis_size("rows")
    Z = 8 if rows % 8 == 0 else 2
    XY = rows // Z
    Y = 4 if XY % 4 == 0 else 1
    X = XY // Y
    N, F = features.shape
    H = weight.shape[1]
    nb = bnd_vals.shape[1]
    nh = hub_vals.shape[1]
    hb = Z * 4
    piece = 2 * F // XY
    K = N + nb + nh
    V = pltpu.VMEM
    D = pltpu.SemaphoreType.DMA
    hbm = pl.BlockSpec(memory_space=pltpu.HBM)
    vm = pl.BlockSpec(memory_space=pltpu.VMEM)
    scratch = [
        V((N, F), F32), V((F, H), F32), V((1, H), F32), V((N, H), F32), V((N, KT * TB), F32),
        pltpu.SMEM((KT, N // TB), jnp.int32), pltpu.SMEM((1, N // TB), jnp.int32),
        pltpu.SMEM((1, 4), jnp.int32),
        V((N, nh), F32), pltpu.SMEM((4, rows), jnp.int32), V((4, rows), jnp.int32), V((N, nb), F32),
        V((N, K), BF16), V((N, K), BF16), V((K, N), BF16), V((K, N), BF16),
        V((H, 2 * F), BF16), V((F, 2 * H), BF16),
        V((4, F), F32), V((rows, 4, F), F32), V((Z, 4, F), F32),
        V((rows, 4, F), F32), V((2, rows, 4, F), F32),
        V((N, F), F32), V((N, H), F32), V((N, 2 * F), BF16),
        V((nh // 2, F), F32), V((nh // 2, F), F32), V((XY, hb, F), F32), V((XY, hb, F), F32),
        V((Z, 4, F), F32), V((Z, 4, F), F32),
        V((rows, 4, F), F32), V((rows, 4, F), F32),
        V((XY, piece, F), F32), V((XY, piece, F), F32), V((2, piece, F), F32), V((piece, F), F32),
        V((Z, piece, F), F32), V((piece, F), F32), V((XY, piece, F), F32),
        D((12,)), D((14,)), D((14,)), pltpu.SemaphoreType.REGULAR((Z,)),
    ]
    results = pl.pallas_call(
        functools.partial(kernel, X, Y, Z),
        out_shape=(pltpu.VMEM((N, H), F32), pltpu.VMEM((F, H), F32), pltpu.VMEM((N, F), F32)),
        in_specs=[hbm] * 11,
        out_specs=(vm, vm, vm),
        scratch_shapes=scratch,
        compiler_params=pltpu.CompilerParams(
            collective_id=0, has_side_effects=True, vmem_limit_bytes=60 * 1024 * 1024
        ),
    )(
        features, weight, bias.reshape(1, H), cotangent, loc_vals, loc_cols.T,
        loc_count.reshape(1, -1), hub_rows.reshape(1, 4), hub_vals,
        send_rows[0].T, bnd_vals,
    )
    return pl.pallas_call(
        write_out,
        out_shape=(
            jax.ShapeDtypeStruct((N, H), F32),
            jax.ShapeDtypeStruct((F, H), F32),
            jax.ShapeDtypeStruct((N, F), F32),
        ),
        in_specs=[vm] * 3,
        out_specs=(pl.BlockSpec(memory_space=pl.ANY),) * 3,
        scratch_shapes=[D((3,))],
        compiler_params=pltpu.CompilerParams(vmem_limit_bytes=4 * 1024 * 1024),
    )(*results)


def solution(mesh):
    node = P(("rows", "grp"), None)
    flat = P(("rows", "grp"))
    return jax.shard_map(
        shards,
        mesh=mesh,
        in_specs=(node, P(), P(), node, node, node, flat, flat, node, P(("rows", "grp"), None, None), node),
        out_specs=(node, P(), node),
        check_vma=False,
    )
```

```python
import functools
import math

import jax
import jax.numpy as jnp
from jax import lax
from jax.experimental import pallas as pl
from jax.experimental.pallas import tpu as pltpu
from jax.sharding import PartitionSpec as P

TB = 64
KT = 4
MESH = pl.DeviceIdType.MESH
F32 = jnp.float32
BF16 = jnp.bfloat16
C0 = math.sqrt(2.0 / math.pi)
C1 = 0.044715


def split(value):
    high = value.astype(BF16)
    low = (value - high.astype(F32)).astype(BF16)
    return high, low


def mm(left, right):
    return jnp.dot(left, right, preferred_element_type=F32)


def wide(value):
    high, low = split(value)
    return jnp.concatenate([high, low], axis=1)


def mm3(high, low, pair):
    n = pair.shape[1] // 2
    both = mm(high, pair)
    return both[:, :n] + both[:, n:] + mm(low, pair[:, :n])


def kernel(
    X, Y, Z,
    feat_h, w_h, b_h, cot_h, lv_h, lcols_h, lcount_h, hrows_h, hv_h, srows_h, bv_h,
    act_o, wg_o, fg_o,
    feat, w, b, cot, lv, lcols, lcount, hrows, hv, srows, srows_v, bv,
    ahi, alo, athi, atlo, wt, wpair,
    hown, s1, h1, br, hub,
    agg, prg, dag,
    gs, gsib, gown, gx, gp, gz,
    bsend, ar,
    ws, wx, wp, wsib, wz, wsum, wall,
    in_sem, ssem, rsem, plane_sem,
):
    r = lax.axis_index("rows")
    g = lax.axis_index("grp")
    xy = r // Z
    z = lax.rem(r, Z)
    XY = X * Y
    R = XY * Z
    F = feat.shape[1]
    N = feat.shape[0]
    nb = bv.shape[1]
    nh = hv.shape[1]
    hb = Z * 4

    loads = {}

    def load(*names):
        for name in names:
            src, dst, i = arrays[name]
            loads[name] = pltpu.make_async_copy(src, dst, in_sem.at[i])
            loads[name].start()

    arrays = {}
    for i, (name, src, dst) in enumerate([
        ("feat", feat_h, feat), ("srows", srows_h, srows), ("hrows", hrows_h, hrows),
        ("lcols", lcols_h, lcols), ("lcount", lcount_h, lcount),
        ("lv", lv_h, lv), ("bv", bv_h, bv), ("hv", hv_h, hv), ("w", w_h, w), ("b", b_h, b),
        ("cot", cot_h, cot), ("srows_v", srows_h, srows_v),
    ]):
        arrays[name] = (src, dst, i)
    load("srows", "hrows", "feat")

    barrier = pltpu.get_barrier_semaphore()
    x = xy // Y
    y = lax.rem(xy, Y)
    z_order = sorted(range(1, Z), key=lambda d: -min(d, Z - d))
    xy_order = sorted(
        ((dx, dy) for dx in range(X) for dy in range(Y)),
        key=lambda d: -min(d[0], X - d[0]) - min(d[1], Y - d[1]))[:-1]

    def zline(d):
        return lax.rem(z + d, Z)

    def plane(d):
        return lax.rem(x + d[0], X) * Y + lax.rem(y + d[1], Y)

    def others(n, own):
        return [jnp.where(own <= i, i + 1, i) for i in range(n - 1)]

    def signal(sem, dev, core):
        pl.semaphore_signal(sem, inc=1, device_id=(dev, core), device_id_type=MESH)

    for d in z_order:
        signal(barrier, xy * Z + zline(d), g)
    for d in xy_order:
        signal(barrier, plane(d) * Z + z, g)
    signal(barrier, r, 1 - g)
    load("lcols", "lcount", "lv", "w", "b", "srows_v")

    loads["hrows"].wait()
    loads["feat"].wait()
    for j in range(4):
        hown[pl.ds(j, 1), :] = feat[pl.ds(hrows[0, j], 1), :]

    pl.semaphore_wait(barrier, (Z - 1) + (XY - 1) + 1)

    for d in z_order:
        signal(plane_sem.at[z], xy * Z + zline(d), g)

    def remote(src, dst, k, dev, core):
        return pltpu.make_async_remote_copy(
            src_ref=src, dst_ref=dst, send_sem=ssem.at[k], recv_sem=rsem.at[k],
            device_id=(dev, core), device_id_type=MESH)

    def wait_recv(ref, k):
        pltpu.make_async_copy(ref, ref, rsem.at[k]).wait()

    def wait_send(ref, k):
        pltpu.make_async_copy(ref, ref, ssem.at[k]).wait()

    def each(order, send):
        def step(d, k, c):
            back = (k + 1) // 2
            dz = lax.rem(Z // 2 + lax.rem(k, 2) * (Z - 2 * back) + back, Z)
            send(plane(d) * Z + zline(dz))
            return c

        for d in order:
            lax.fori_loop(0, Z, functools.partial(step, d), 0)

    def rest(send):
        for d in z_order:
            send(xy * Z + zline(d))

    first, second = xy_order[:11], xy_order[11:]

    def send_bnd(p):
        remote(s1.at[p], br.at[r], 3, p, g).start()

    for d in z_order:
        remote(hown, h1.at[z], 0, xy * Z + zline(d), g).start()
    pltpu.make_async_copy(hown, h1.at[z], rsem.at[0]).start()

    loads["srows"].wait()

    def pack(i, c):
        for j in range(4):
            s1[i, pl.ds(j, 1), :] = feat[pl.ds(srows[j, i], 1), :]
        return c

    lax.fori_loop(0, R, pack, 0, unroll=4)
    load("bv", "hv", "cot")
    pltpu.make_async_copy(s1.at[r], br.at[r], rsem.at[3]).start()
    for d in xy_order:
        send_bnd(plane(d) * Z + z)

    for pair in range(1, Z // 2 + 1):
        for d in sorted({pair, Z - pair}):
            pl.semaphore_wait(plane_sem.at[zline(d)], 1)
        for dxy in xy_order + [(0, 0)]:
            for d in sorted({pair, Z - pair}):
                send_bnd(plane(dxy) * Z + zline(d))
    wait_recv(h1, 0)
    for d in xy_order:
        remote(h1, hub.at[g, pl.ds(xy * Z, Z)], 2, plane(d) * Z + z, g).start()
    pltpu.make_async_copy(h1, hub.at[g, pl.ds(xy * Z, Z)], rsem.at[2]).start()

    loads["lcols"].wait()
    loads["lcount"].wait()
    loads["lv"].wait()
    lane = lax.broadcasted_iota(jnp.int32, (TB, 2 * TB), 1)
    upper = lane >= TB
    for t in range(N // TB):
        rows = pl.ds(t * TB, TB)
        dup = []
        for pair in range(KT // 2):
            v = lv[rows, pl.ds(pair * 2 * TB, 2 * TB)]
            turned = pltpu.roll(v, TB, 1)
            dup.append(jnp.where(upper, turned, v))
            dup.append(jnp.where(upper, v, turned))
        cols = [jnp.where(k < lcount[0, t], lcols[k, t], -1) for k in range(KT)]
        for c in range(N // (2 * TB)):
            tile = jnp.where(upper, 2 * c + 1, 2 * c)
            out = jnp.zeros((TB, 2 * TB), F32)
            for k in range(KT):
                out = jnp.where(tile == cols[k], dup[k], out)
            high, low = split(out)
            ahi[rows, pl.ds(c * 2 * TB, 2 * TB)] = high
            alo[rows, pl.ds(c * 2 * TB, 2 * TB)] = low

    agg[...] = mm3(ahi[:, :N], alo[:, :N], wide(feat[...]))
    for c in range(N // 128):
        cols = pl.ds(c * 128, 128)
        athi[cols, :] = ahi[:, cols].astype(F32).T.astype(BF16)
        atlo[cols, :] = alo[:, cols].astype(F32).T.astype(BF16)

    loads["w"].wait()
    wv = w[...]
    wpair[...] = wide(wv)
    wt[...] = wide(wv.T)

    loads["bv"].wait()
    step = min(128, nb)
    for c in range(nb // step):
        v = bv[:, pl.ds(c * step, step)]
        high, low = split(v)
        ahi[:, pl.ds(N + c * step, step)] = high
        alo[:, pl.ds(N + c * step, step)] = low
        high, low = split(v.T)
        athi[pl.ds(N + c * step, step), :] = high
        atlo[pl.ds(N + c * step, step), :] = low

    loads["hv"].wait()
    step = min(128, nh)
    for c in range(nh // step):
        v = hv[:, pl.ds(c * step, step)]
        high, low = split(v)
        ahi[:, pl.ds(N + nb + c * step, step)] = high
        alo[:, pl.ds(N + nb + c * step, step)] = low
        turned = v.T.reshape(step // 8, 8, N)
        for core in range(2):
            high, low = split(turned[:, core * 4:core * 4 + 4, :].reshape(step // 2, N))
            to = pl.ds(N + nb + core * (nh // 2) + c * (step // 2), step // 2)
            athi[to, :] = high
            atlo[to, :] = low

    wait_recv(hub.at[g], 2)
    to_sib = remote(hub.at[g], hub.at[g], 4, r, 1 - g)
    to_sib.start()
    to_sib.wait_recv()
    vh = jnp.concatenate([hub[0], hub[1]], axis=1).reshape(nh, F)
    agg[...] += mm3(ahi[:, N + nb:], alo[:, N + nb:], wide(vh))
    wait_recv(br, 3)
    vb = br[...].reshape(nb, F)
    agg[...] += mm3(ahi[:, N:N + nb], alo[:, N:N + nb], wide(vb))

    loads["b"].wait()
    loads["cot"].wait()
    H = w.shape[1]
    step = 128
    wsplit = wpair[...]
    for c in range(N // step):
        rows = pl.ds(c * step, step)
        high, low = split(agg[rows, :])
        both = mm(high, wsplit)
        v = both[:, :H] + both[:, H:] + mm(low, wsplit[:, :H]) + b[...]
        sq = v * v
        t = jnp.tanh(C0 * (v + C1 * (sq * v)))
        act_o[rows, :] = 0.5 * v * (1.0 + t)
        slope = 0.5 * (1.0 + t) + 0.5 * v * (1.0 - t * t) * (C0 * (1.0 + 3.0 * C1 * sq))
        prg[rows, :] = cot[rows, :] * slope
    ahigh, alow = split(agg[...].T)
    wh, wl = split(prg[...])
    wterm = mm(ahigh, wh) + mm(ahigh, wl) + mm(alow, wh)
    ws[...] = jnp.concatenate([wterm[:, :F], wterm[:, F:]], axis=0).reshape(ws.shape)
    for d in xy_order:
        remote(ws.at[plane(d)], wx.at[xy], 8, plane(d) * Z + z, g).start()
    pltpu.make_async_copy(ws.at[xy], wx.at[xy], rsem.at[8]).start()

    high, low = split(prg[...])
    dag[...] = wide(mm3(high, low, wt[...]))

    g2 = dag[...]

    def back(start, size):
        return mm3(athi[pl.ds(start, size), :], atlo[pl.ds(start, size), :], g2)

    hbase = N + nb
    gs[...] = back(hbase + (1 - g) * (nh // 2), nh // 2)
    hub_sib = remote(gs, gsib, 5, r, 1 - g)
    hub_sib.start()
    own = back(hbase + g * (nh // 2), nh // 2)
    bsend[...] = back(N, nb).reshape(R, 4, F)
    hub_sib.wait_recv()
    gown[...] = (own + gsib[...]).reshape(XY, hb, F)
    for d in xy_order:
        remote(gown.at[plane(d)], gx.at[xy], 7, plane(d) * Z + z, g).start()
    pltpu.make_async_copy(gown.at[xy], gx.at[xy], rsem.at[7]).start()

    def send_back(p):
        remote(bsend.at[p], ar.at[r], 6, p, g).start()

    pltpu.make_async_copy(bsend.at[r], ar.at[r], rsem.at[6]).start()
    each(first, send_back)

    wait_recv(wx, 8)
    total = wx[0]
    for i in range(1, XY):
        total += wx[i]
    wp[0] = total
    w_sib = remote(wp.at[0], wsib, 12, r, 1 - g)
    w_sib.start()
    w_sib.wait_recv()
    wp[1] = total + wsib[...]
    for p in others(Z, z):
        remote(wp.at[1], wz.at[z], 11, xy * Z + p, g).start()
    pltpu.make_async_copy(wp.at[1], wz.at[z], rsem.at[11]).start()

    each(second, send_back)
    rest(send_back)

    fg_o[...] = back(0, N)

    wait_recv(gx, 7)
    total = gx[0]
    for i in range(1, XY):
        total += gx[i]
    gp[...] = total.reshape(Z, 4, F)
    for p in others(Z, z):
        remote(gp.at[p], gz.at[z], 10, xy * Z + p, g).start()
    pltpu.make_async_copy(gp.at[z], gz.at[z], rsem.at[10]).start()

    wait_recv(wz, 11)
    total = wz[0]
    for i in range(1, Z):
        total += wz[i]
    wsum[...] = total

    for p in others(XY, xy):
        remote(wsum, wall.at[xy], 13, p * Z + z, g).start()
    pltpu.make_async_copy(wsum, wall.at[xy], rsem.at[13]).start()

    loads["srows_v"].wait()
    node = lax.broadcasted_iota(jnp.int32, (N, R), 0)
    picks = [jnp.where(node == srows_v[pl.ds(j, 1), :], 1.0, 0.0).astype(BF16) for j in range(4)]
    pick = jnp.concatenate(picks, axis=1)
    wait_recv(ar, 6)
    arr = jnp.concatenate([ar[:, j, :] for j in range(4)], axis=0)
    both = mm(pick, wide(arr))
    fg_o[...] += both[:, :F] + both[:, F:]

    wait_recv(gz, 10)
    total = gz[0]
    for i in range(1, Z):
        total += gz[i]
    node = lax.broadcasted_iota(jnp.int32, (N, F), 0)
    for j in range(4):
        fg_o[...] += jnp.where(node == hrows[0, j], total[j:j + 1, :], 0.0)

    wait_recv(wall, 13)
    full = wall[...].reshape(2 * F, F) * float((R * 2 * N) ** -0.5)
    wg_o[:, :F] = full[:F]
    wg_o[:, F:] = full[F:]

    wait_send(h1.at[pl.ds(0, Z - 1)], 0)
    wait_send(hub.at[0, pl.ds(0, (XY - 1) * Z)], 2)
    wait_send(br.at[pl.ds(0, R - 1)], 3)
    to_sib.wait_send()
    hub_sib.wait_send()
    wait_send(ar.at[pl.ds(0, R - 1)], 6)
    wait_send(gown.at[pl.ds(0, XY - 1)], 7)
    wait_send(wx.at[pl.ds(0, XY - 1)], 8)

    wait_send(gz.at[pl.ds(0, Z - 1)], 10)
    wait_send(wz.at[pl.ds(0, Z - 1)], 11)
    w_sib.wait_send()
    wait_send(wall.at[pl.ds(0, XY - 1)], 13)


def write_out(a_ref, b_ref, c_ref, a_out, b_out, c_out, sems):
    copies = [
        pltpu.make_async_copy(a_ref, a_out, sems.at[0]),
        pltpu.make_async_copy(b_ref, b_out, sems.at[1]),
        pltpu.make_async_copy(c_ref, c_out, sems.at[2]),
    ]
    for copy in copies:
        copy.start()
    for copy in copies:
        copy.wait()


def shards(features, weight, bias, cotangent, loc_vals, loc_cols, loc_count, hub_rows, hub_vals, send_rows, bnd_vals):
    rows = lax.axis_size("rows")
    Z = 8 if rows % 8 == 0 else 2
    XY = rows // Z
    Y = 4 if XY % 4 == 0 else 1
    X = XY // Y
    N, F = features.shape
    H = weight.shape[1]
    nb = bnd_vals.shape[1]
    nh = hub_vals.shape[1]
    hb = Z * 4
    piece = 2 * F // XY
    K = N + nb + nh
    V = pltpu.VMEM
    D = pltpu.SemaphoreType.DMA
    hbm = pl.BlockSpec(memory_space=pltpu.HBM)
    vm = pl.BlockSpec(memory_space=pltpu.VMEM)
    scratch = [
        V((N, F), F32), V((F, H), F32), V((1, H), F32), V((N, H), F32), V((N, KT * TB), F32),
        pltpu.SMEM((KT, N // TB), jnp.int32), pltpu.SMEM((1, N // TB), jnp.int32),
        pltpu.SMEM((1, 4), jnp.int32),
        V((N, nh), F32), pltpu.SMEM((4, rows), jnp.int32), V((4, rows), jnp.int32), V((N, nb), F32),
        V((N, K), BF16), V((N, K), BF16), V((K, N), BF16), V((K, N), BF16),
        V((H, 2 * F), BF16), V((F, 2 * H), BF16),
        V((4, F), F32), V((rows, 4, F), F32), V((Z, 4, F), F32),
        V((rows, 4, F), F32), V((2, rows, 4, F), F32),
        V((N, F), F32), V((N, H), F32), V((N, 2 * F), BF16),
        V((nh // 2, F), F32), V((nh // 2, F), F32), V((XY, hb, F), F32), V((XY, hb, F), F32),
        V((Z, 4, F), F32), V((Z, 4, F), F32),
        V((rows, 4, F), F32), V((rows, 4, F), F32),
        V((XY, piece, F), F32), V((XY, piece, F), F32), V((2, piece, F), F32), V((piece, F), F32),
        V((Z, piece, F), F32), V((piece, F), F32), V((XY, piece, F), F32),
        D((12,)), D((14,)), D((14,)), pltpu.SemaphoreType.REGULAR((Z,)),
    ]
    results = pl.pallas_call(
        functools.partial(kernel, X, Y, Z),
        out_shape=(pltpu.VMEM((N, H), F32), pltpu.VMEM((F, H), F32), pltpu.VMEM((N, F), F32)),
        in_specs=[hbm] * 11,
        out_specs=(vm, vm, vm),
        scratch_shapes=scratch,
        compiler_params=pltpu.CompilerParams(
            collective_id=0, has_side_effects=True, vmem_limit_bytes=60 * 1024 * 1024
        ),
    )(
        features, weight, bias.reshape(1, H), cotangent, loc_vals, loc_cols.T,
        loc_count.reshape(1, -1), hub_rows.reshape(1, 4), hub_vals,
        send_rows[0].T, bnd_vals,
    )
    return pl.pallas_call(
        write_out,
        out_shape=(
            jax.ShapeDtypeStruct((N, H), F32),
            jax.ShapeDtypeStruct((F, H), F32),
            jax.ShapeDtypeStruct((N, F), F32),
        ),
        in_specs=[vm] * 3,
        out_specs=(pl.BlockSpec(memory_space=pl.ANY),) * 3,
        scratch_shapes=[D((3,))],
        compiler_params=pltpu.CompilerParams(vmem_limit_bytes=4 * 1024 * 1024),
    )(*results)


def solution(mesh):
    node = P(("rows", "grp"), None)
    flat = P(("rows", "grp"))
    return jax.shard_map(
        shards,
        mesh=mesh,
        in_specs=(node, P(), P(), node, node, node, flat, flat, node, P(("rows", "grp"), None, None), node),
        out_specs=(node, P(), node),
        check_vma=False,
    )
```

```python
import functools
import math

import jax
import jax.numpy as jnp
from jax import lax
from jax.experimental import pallas as pl
from jax.experimental.pallas import tpu as pltpu
from jax.sharding import PartitionSpec as P

TB = 64
KT = 4
MESH = pl.DeviceIdType.MESH
F32 = jnp.float32
BF16 = jnp.bfloat16
C0 = math.sqrt(2.0 / math.pi)
C1 = 0.044715


def split(value):
    high = value.astype(BF16)
    low = (value - high.astype(F32)).astype(BF16)
    return high, low


def mm(left, right):
    return jnp.dot(left, right, preferred_element_type=F32)


def wide(value):
    high, low = split(value)
    return jnp.concatenate([high, low], axis=1)


def mm3(high, low, pair):
    n = pair.shape[1] // 2
    both = mm(high, pair)
    return both[:, :n] + both[:, n:] + mm(low, pair[:, :n])


def kernel(
    X, Y, Z,
    feat_h, w_h, b_h, cot_h, lv_h, lcols_h, lcount_h, hrows_h, hv_h, srows_h, bv_h,
    act_o, wg_o, fg_o,
    feat, w, b, cot, lv, lcols, lcount, hrows, hv, srows, srows_v, bv,
    ahi, alo, athi, atlo, wt, wpair,
    hown, s1, h1, br, hub,
    agg, prg, dag,
    gs, gsib, gown, gx, gp, gz,
    bsend, ar,
    ws, wx, wp, wsib, wz, wsum, wall,
    in_sem, ssem, rsem, plane_sem,
):
    r = lax.axis_index("rows")
    g = lax.axis_index("grp")
    xy = r // Z
    z = lax.rem(r, Z)
    XY = X * Y
    R = XY * Z
    F = feat.shape[1]
    N = feat.shape[0]
    nb = bv.shape[1]
    nh = hv.shape[1]
    hb = Z * 4

    loads = {}

    def load(*names):
        for name in names:
            src, dst, i = arrays[name]
            loads[name] = pltpu.make_async_copy(src, dst, in_sem.at[i])
            loads[name].start()

    arrays = {}
    for i, (name, src, dst) in enumerate([
        ("feat", feat_h, feat), ("srows", srows_h, srows), ("hrows", hrows_h, hrows),
        ("lcols", lcols_h, lcols), ("lcount", lcount_h, lcount),
        ("lv", lv_h, lv), ("bv", bv_h, bv), ("hv", hv_h, hv), ("w", w_h, w), ("b", b_h, b),
        ("cot", cot_h, cot), ("srows_v", srows_h, srows_v),
    ]):
        arrays[name] = (src, dst, i)
    load("srows", "hrows", "feat")

    barrier = pltpu.get_barrier_semaphore()
    x = xy // Y
    y = lax.rem(xy, Y)
    z_order = sorted(range(1, Z), key=lambda d: -min(d, Z - d))
    xy_order = sorted(
        ((dx, dy) for dx in range(X) for dy in range(Y)),
        key=lambda d: -min(d[0], X - d[0]) - min(d[1], Y - d[1]))[:-1]

    def zline(d):
        return lax.rem(z + d, Z)

    def plane(d):
        return lax.rem(x + d[0], X) * Y + lax.rem(y + d[1], Y)

    def others(n, own):
        return [jnp.where(own <= i, i + 1, i) for i in range(n - 1)]

    def signal(sem, dev, core):
        pl.semaphore_signal(sem, inc=1, device_id=(dev, core), device_id_type=MESH)

    for d in z_order:
        signal(barrier, xy * Z + zline(d), g)
    for d in xy_order:
        signal(barrier, plane(d) * Z + z, g)
    signal(barrier, r, 1 - g)
    load("lcols", "lcount", "lv", "w", "b", "srows_v")

    loads["hrows"].wait()
    loads["feat"].wait()
    for j in range(4):
        hown[pl.ds(j, 1), :] = feat[pl.ds(hrows[0, j], 1), :]

    pl.semaphore_wait(barrier, (Z - 1) + (XY - 1) + 1)

    for d in z_order:
        signal(plane_sem.at[z], xy * Z + zline(d), g)

    def remote(src, dst, k, dev, core):
        return pltpu.make_async_remote_copy(
            src_ref=src, dst_ref=dst, send_sem=ssem.at[k], recv_sem=rsem.at[k],
            device_id=(dev, core), device_id_type=MESH)

    def wait_recv(ref, k):
        pltpu.make_async_copy(ref, ref, rsem.at[k]).wait()

    def wait_send(ref, k):
        pltpu.make_async_copy(ref, ref, ssem.at[k]).wait()

    def each(order, send):
        def step(d, k, c):
            back = (k + 1) // 2
            dz = lax.rem(Z // 2 + lax.rem(k, 2) * (Z - 2 * back) + back, Z)
            send(plane(d) * Z + zline(dz))
            return c

        for d in order:
            lax.fori_loop(0, Z, functools.partial(step, d), 0)

    def rest(send):
        for d in z_order:
            send(xy * Z + zline(d))

    first, second = xy_order[:11], xy_order[11:]

    def send_bnd(p):
        remote(s1.at[p], br.at[r], 3, p, g).start()

    for d in z_order:
        remote(hown, h1.at[z], 0, xy * Z + zline(d), g).start()
    pltpu.make_async_copy(hown, h1.at[z], rsem.at[0]).start()

    loads["srows"].wait()

    def pack(i, c):
        for j in range(4):
            s1[i, pl.ds(j, 1), :] = feat[pl.ds(srows[j, i], 1), :]
        return c

    lax.fori_loop(0, R, pack, 0, unroll=4)
    load("bv", "hv", "cot")
    pltpu.make_async_copy(s1.at[r], br.at[r], rsem.at[3]).start()
    for d in xy_order:
        send_bnd(plane(d) * Z + z)

    for pair in range(1, Z // 2 + 1):
        for d in sorted({pair, Z - pair}):
            pl.semaphore_wait(plane_sem.at[zline(d)], 1)
        for dxy in xy_order + [(0, 0)]:
            for d in sorted({pair, Z - pair}):
                send_bnd(plane(dxy) * Z + zline(d))
    wait_recv(h1, 0)
    for d in xy_order:
        remote(h1, hub.at[g, pl.ds(xy * Z, Z)], 2, plane(d) * Z + z, g).start()
    pltpu.make_async_copy(h1, hub.at[g, pl.ds(xy * Z, Z)], rsem.at[2]).start()

    loads["lcols"].wait()
    loads["lcount"].wait()
    loads["lv"].wait()
    lane = lax.broadcasted_iota(jnp.int32, (TB, 2 * TB), 1)
    upper = lane >= TB
    for t in range(N // TB):
        rows = pl.ds(t * TB, TB)
        dup = []
        for pair in range(KT // 2):
            v = lv[rows, pl.ds(pair * 2 * TB, 2 * TB)]
            turned = pltpu.roll(v, TB, 1)
            dup.append(jnp.where(upper, turned, v))
            dup.append(jnp.where(upper, v, turned))
        cols = [jnp.where(k < lcount[0, t], lcols[k, t], -1) for k in range(KT)]
        for c in range(N // (2 * TB)):
            tile = jnp.where(upper, 2 * c + 1, 2 * c)
            out = jnp.zeros((TB, 2 * TB), F32)
            for k in range(KT):
                out = jnp.where(tile == cols[k], dup[k], out)
            high, low = split(out)
            ahi[rows, pl.ds(c * 2 * TB, 2 * TB)] = high
            alo[rows, pl.ds(c * 2 * TB, 2 * TB)] = low

    agg[...] = mm3(ahi[:, :N], alo[:, :N], wide(feat[...]))
    for c in range(N // 128):
        cols = pl.ds(c * 128, 128)
        athi[cols, :] = ahi[:, cols].astype(F32).T.astype(BF16)
        atlo[cols, :] = alo[:, cols].astype(F32).T.astype(BF16)

    loads["w"].wait()
    wv = w[...]
    wpair[...] = wide(wv)
    wt[...] = wide(wv.T)

    loads["bv"].wait()
    step = min(128, nb)
    for c in range(nb // step):
        v = bv[:, pl.ds(c * step, step)]
        high, low = split(v)
        ahi[:, pl.ds(N + c * step, step)] = high
        alo[:, pl.ds(N + c * step, step)] = low
        high, low = split(v.T)
        athi[pl.ds(N + c * step, step), :] = high
        atlo[pl.ds(N + c * step, step), :] = low

    loads["hv"].wait()
    step = min(128, nh)
    for c in range(nh // step):
        v = hv[:, pl.ds(c * step, step)]
        high, low = split(v)
        ahi[:, pl.ds(N + nb + c * step, step)] = high
        alo[:, pl.ds(N + nb + c * step, step)] = low
        turned = v.T.reshape(step // 8, 8, N)
        for core in range(2):
            high, low = split(turned[:, core * 4:core * 4 + 4, :].reshape(step // 2, N))
            to = pl.ds(N + nb + core * (nh // 2) + c * (step // 2), step // 2)
            athi[to, :] = high
            atlo[to, :] = low

    wait_recv(hub.at[g], 2)
    to_sib = remote(hub.at[g], hub.at[g], 4, r, 1 - g)
    to_sib.start()
    to_sib.wait_recv()
    vh = jnp.concatenate([hub[0], hub[1]], axis=1).reshape(nh, F)
    agg[...] += mm3(ahi[:, N + nb:], alo[:, N + nb:], wide(vh))
    wait_recv(br, 3)
    vb = br[...].reshape(nb, F)
    agg[...] += mm3(ahi[:, N:N + nb], alo[:, N:N + nb], wide(vb))

    loads["b"].wait()
    loads["cot"].wait()
    H = w.shape[1]
    step = N // 4
    wsplit = wpair[...]
    wterm = jnp.zeros((F, H), F32)
    for c in range(4):
        rows = pl.ds(c * step, step)
        part = agg[rows, :]
        high, low = split(part)
        both = mm(high, wsplit)
        v = both[:, :H] + both[:, H:] + mm(low, wsplit[:, :H]) + b[...]
        sq = v * v
        t = jnp.tanh(C0 * (v + C1 * (sq * v)))
        act_o[rows, :] = 0.5 * v * (1.0 + t)
        slope = 0.5 * (1.0 + t) + 0.5 * v * (1.0 - t * t) * (C0 * (1.0 + 3.0 * C1 * sq))
        grad = cot[rows, :] * slope
        prg[rows, :] = grad
        ahigh, alow = split(part.T)
        wh, wl = split(grad)
        wterm += mm(ahigh, wh) + mm(ahigh, wl) + mm(alow, wh)

    ws[...] = jnp.concatenate([wterm[:, :F], wterm[:, F:]], axis=0).reshape(ws.shape)
    for d in xy_order:
        remote(ws.at[plane(d)], wx.at[xy], 8, plane(d) * Z + z, g).start()
    pltpu.make_async_copy(ws.at[xy], wx.at[xy], rsem.at[8]).start()

    high, low = split(prg[...])
    dag[...] = wide(mm3(high, low, wt[...]))

    g2 = dag[...]

    def back(start, size):
        return mm3(athi[pl.ds(start, size), :], atlo[pl.ds(start, size), :], g2)

    hbase = N + nb
    gs[...] = back(hbase + (1 - g) * (nh // 2), nh // 2)
    hub_sib = remote(gs, gsib, 5, r, 1 - g)
    hub_sib.start()
    own = back(hbase + g * (nh // 2), nh // 2)
    bsend[...] = back(N, nb).reshape(R, 4, F)
    hub_sib.wait_recv()
    gown[...] = (own + gsib[...]).reshape(XY, hb, F)
    for d in xy_order:
        remote(gown.at[plane(d)], gx.at[xy], 7, plane(d) * Z + z, g).start()
    pltpu.make_async_copy(gown.at[xy], gx.at[xy], rsem.at[7]).start()

    def send_back(p):
        remote(bsend.at[p], ar.at[r], 6, p, g).start()

    pltpu.make_async_copy(bsend.at[r], ar.at[r], rsem.at[6]).start()
    each(first, send_back)

    wait_recv(wx, 8)
    total = wx[0]
    for i in range(1, XY):
        total += wx[i]
    wp[0] = total
    w_sib = remote(wp.at[0], wsib, 12, r, 1 - g)
    w_sib.start()
    w_sib.wait_recv()
    wp[1] = total + wsib[...]
    for p in others(Z, z):
        remote(wp.at[1], wz.at[z], 11, xy * Z + p, g).start()
    pltpu.make_async_copy(wp.at[1], wz.at[z], rsem.at[11]).start()

    each(second, send_back)
    rest(send_back)

    fg_o[...] = back(0, N)

    wait_recv(gx, 7)
    total = gx[0]
    for i in range(1, XY):
        total += gx[i]
    gp[...] = total.reshape(Z, 4, F)
    for p in others(Z, z):
        remote(gp.at[p], gz.at[z], 10, xy * Z + p, g).start()
    pltpu.make_async_copy(gp.at[z], gz.at[z], rsem.at[10]).start()

    wait_recv(wz, 11)
    total = wz[0]
    for i in range(1, Z):
        total += wz[i]
    wsum[...] = total

    for p in others(XY, xy):
        remote(wsum, wall.at[xy], 13, p * Z + z, g).start()
    pltpu.make_async_copy(wsum, wall.at[xy], rsem.at[13]).start()

    loads["srows_v"].wait()
    node = lax.broadcasted_iota(jnp.int32, (N, R), 0)
    picks = [jnp.where(node == srows_v[pl.ds(j, 1), :], 1.0, 0.0).astype(BF16) for j in range(4)]
    pick = jnp.concatenate(picks, axis=1)
    wait_recv(ar, 6)
    arr = jnp.concatenate([ar[:, j, :] for j in range(4)], axis=0)
    both = mm(pick, wide(arr))
    fg_o[...] += both[:, :F] + both[:, F:]

    wait_recv(gz, 10)
    total = gz[0]
    for i in range(1, Z):
        total += gz[i]
    node = lax.broadcasted_iota(jnp.int32, (N, F), 0)
    for j in range(4):
        fg_o[...] += jnp.where(node == hrows[0, j], total[j:j + 1, :], 0.0)

    wait_recv(wall, 13)
    full = wall[...].reshape(2 * F, F) * float((R * 2 * N) ** -0.5)
    wg_o[:, :F] = full[:F]
    wg_o[:, F:] = full[F:]

    wait_send(h1.at[pl.ds(0, Z - 1)], 0)
    wait_send(hub.at[0, pl.ds(0, (XY - 1) * Z)], 2)
    wait_send(br.at[pl.ds(0, R - 1)], 3)
    to_sib.wait_send()
    hub_sib.wait_send()
    wait_send(ar.at[pl.ds(0, R - 1)], 6)
    wait_send(gown.at[pl.ds(0, XY - 1)], 7)
    wait_send(wx.at[pl.ds(0, XY - 1)], 8)

    wait_send(gz.at[pl.ds(0, Z - 1)], 10)
    wait_send(wz.at[pl.ds(0, Z - 1)], 11)
    w_sib.wait_send()
    wait_send(wall.at[pl.ds(0, XY - 1)], 13)


def write_out(a_ref, b_ref, c_ref, a_out, b_out, c_out, sems):
    copies = [
        pltpu.make_async_copy(a_ref, a_out, sems.at[0]),
        pltpu.make_async_copy(b_ref, b_out, sems.at[1]),
        pltpu.make_async_copy(c_ref, c_out, sems.at[2]),
    ]
    for copy in copies:
        copy.start()
    for copy in copies:
        copy.wait()


def shards(features, weight, bias, cotangent, loc_vals, loc_cols, loc_count, hub_rows, hub_vals, send_rows, bnd_vals):
    rows = lax.axis_size("rows")
    Z = 8 if rows % 8 == 0 else 2
    XY = rows // Z
    Y = 4 if XY % 4 == 0 else 1
    X = XY // Y
    N, F = features.shape
    H = weight.shape[1]
    nb = bnd_vals.shape[1]
    nh = hub_vals.shape[1]
    hb = Z * 4
    piece = 2 * F // XY
    K = N + nb + nh
    V = pltpu.VMEM
    D = pltpu.SemaphoreType.DMA
    hbm = pl.BlockSpec(memory_space=pltpu.HBM)
    vm = pl.BlockSpec(memory_space=pltpu.VMEM)
    scratch = [
        V((N, F), F32), V((F, H), F32), V((1, H), F32), V((N, H), F32), V((N, KT * TB), F32),
        pltpu.SMEM((KT, N // TB), jnp.int32), pltpu.SMEM((1, N // TB), jnp.int32),
        pltpu.SMEM((1, 4), jnp.int32),
        V((N, nh), F32), pltpu.SMEM((4, rows), jnp.int32), V((4, rows), jnp.int32), V((N, nb), F32),
        V((N, K), BF16), V((N, K), BF16), V((K, N), BF16), V((K, N), BF16),
        V((H, 2 * F), BF16), V((F, 2 * H), BF16),
        V((4, F), F32), V((rows, 4, F), F32), V((Z, 4, F), F32),
        V((rows, 4, F), F32), V((2, rows, 4, F), F32),
        V((N, F), F32), V((N, H), F32), V((N, 2 * F), BF16),
        V((nh // 2, F), F32), V((nh // 2, F), F32), V((XY, hb, F), F32), V((XY, hb, F), F32),
        V((Z, 4, F), F32), V((Z, 4, F), F32),
        V((rows, 4, F), F32), V((rows, 4, F), F32),
        V((XY, piece, F), F32), V((XY, piece, F), F32), V((2, piece, F), F32), V((piece, F), F32),
        V((Z, piece, F), F32), V((piece, F), F32), V((XY, piece, F), F32),
        D((12,)), D((14,)), D((14,)), pltpu.SemaphoreType.REGULAR((Z,)),
    ]
    results = pl.pallas_call(
        functools.partial(kernel, X, Y, Z),
        out_shape=(pltpu.VMEM((N, H), F32), pltpu.VMEM((F, H), F32), pltpu.VMEM((N, F), F32)),
        in_specs=[hbm] * 11,
        out_specs=(vm, vm, vm),
        scratch_shapes=scratch,
        compiler_params=pltpu.CompilerParams(
            collective_id=0, has_side_effects=True, vmem_limit_bytes=60 * 1024 * 1024
        ),
    )(
        features, weight, bias.reshape(1, H), cotangent, loc_vals, loc_cols.T,
        loc_count.reshape(1, -1), hub_rows.reshape(1, 4), hub_vals,
        send_rows[0].T, bnd_vals,
    )
    return pl.pallas_call(
        write_out,
        out_shape=(
            jax.ShapeDtypeStruct((N, H), F32),
            jax.ShapeDtypeStruct((F, H), F32),
            jax.ShapeDtypeStruct((N, F), F32),
        ),
        in_specs=[vm] * 3,
        out_specs=(pl.BlockSpec(memory_space=pl.ANY),) * 3,
        scratch_shapes=[D((3,))],
        compiler_params=pltpu.CompilerParams(vmem_limit_bytes=4 * 1024 * 1024),
    )(*results)


def solution(mesh):
    node = P(("rows", "grp"), None)
    flat = P(("rows", "grp"))
    return jax.shard_map(
        shards,
        mesh=mesh,
        in_specs=(node, P(), P(), node, node, node, flat, flat, node, P(("rows", "grp"), None, None), node),
        out_specs=(node, P(), node),
        check_vma=False,
    )
```

```python
import functools
import math

import jax
import jax.numpy as jnp
from jax import lax
from jax.experimental import pallas as pl
from jax.experimental.pallas import tpu as pltpu
from jax.sharding import PartitionSpec as P

TB = 64
KT = 4
MESH = pl.DeviceIdType.MESH
F32 = jnp.float32
BF16 = jnp.bfloat16
C0 = math.sqrt(2.0 / math.pi)
C1 = 0.044715


def split(value):
    high = value.astype(BF16)
    low = (value - high.astype(F32)).astype(BF16)
    return high, low


def mm(left, right):
    return jnp.dot(left, right, preferred_element_type=F32)


def wide(value):
    high, low = split(value)
    return jnp.concatenate([high, low], axis=1)


def mm3(high, low, pair):
    n = pair.shape[1] // 2
    both = mm(high, pair)
    return both[:, :n] + both[:, n:] + mm(low, pair[:, :n])


def kernel(
    X, Y, Z,
    feat_h, w_h, b_h, cot_h, lv_h, lcols_h, lcount_h, hrows_h, hv_h, srows_h, bv_h,
    act_o, wg_o, fg_o,
    feat, w, b, cot, lv, lcols, lcount, hrows, hv, srows, srows_v, bv,
    ahi, alo, athi, atlo, wt, wpair,
    hown, s1, h1, br, hub,
    agg, prg, dag,
    gs, gsib, gown, gx, gp, gz,
    bsend, ar,
    ws, wx, wp, wsib, wz, wsum, wall,
    in_sem, ssem, rsem, plane_sem,
):
    r = lax.axis_index("rows")
    g = lax.axis_index("grp")
    xy = r // Z
    z = lax.rem(r, Z)
    XY = X * Y
    R = XY * Z
    F = feat.shape[1]
    N = feat.shape[0]
    nb = bv.shape[1]
    nh = hv.shape[1]
    hb = Z * 4

    loads = {}

    def load(*names):
        for name in names:
            src, dst, i = arrays[name]
            loads[name] = pltpu.make_async_copy(src, dst, in_sem.at[i])
            loads[name].start()

    arrays = {}
    for i, (name, src, dst) in enumerate([
        ("feat", feat_h, feat), ("srows", srows_h, srows), ("hrows", hrows_h, hrows),
        ("lcols", lcols_h, lcols), ("lcount", lcount_h, lcount),
        ("lv", lv_h, lv), ("bv", bv_h, bv), ("hv", hv_h, hv), ("w", w_h, w), ("b", b_h, b),
        ("cot", cot_h, cot), ("srows_v", srows_h, srows_v),
    ]):
        arrays[name] = (src, dst, i)
    barrier = pltpu.get_barrier_semaphore()
    x = xy // Y
    y = lax.rem(xy, Y)
    z_order = sorted(range(1, Z), key=lambda d: -min(d, Z - d))
    xy_order = sorted(
        ((dx, dy) for dx in range(X) for dy in range(Y)),
        key=lambda d: -min(d[0], X - d[0]) - min(d[1], Y - d[1]))[:-1]

    def zline(d):
        return lax.rem(z + d, Z)

    def plane(d):
        return lax.rem(x + d[0], X) * Y + lax.rem(y + d[1], Y)

    def others(n, own):
        return [jnp.where(own <= i, i + 1, i) for i in range(n - 1)]

    def signal(sem, dev, core):
        pl.semaphore_signal(sem, inc=1, device_id=(dev, core), device_id_type=MESH)

    for d in z_order:
        signal(barrier, xy * Z + zline(d), g)
    for d in xy_order:
        signal(barrier, plane(d) * Z + z, g)
    signal(barrier, r, 1 - g)
    load("hrows", "feat", "srows")
    load("lcols", "lcount", "lv", "w", "b", "srows_v")

    pl.semaphore_wait(barrier, (Z - 1) + (XY - 1) + 1)

    for d in z_order:
        signal(plane_sem.at[z], xy * Z + zline(d), g)

    loads["hrows"].wait()
    loads["feat"].wait()
    for j in range(4):
        hown[pl.ds(j, 1), :] = feat[pl.ds(hrows[0, j], 1), :]

    def remote(src, dst, k, dev, core):
        return pltpu.make_async_remote_copy(
            src_ref=src, dst_ref=dst, send_sem=ssem.at[k], recv_sem=rsem.at[k],
            device_id=(dev, core), device_id_type=MESH)

    def wait_recv(ref, k):
        pltpu.make_async_copy(ref, ref, rsem.at[k]).wait()

    def wait_send(ref, k):
        pltpu.make_async_copy(ref, ref, ssem.at[k]).wait()

    def each(order, send):
        def step(d, k, c):
            back = (k + 1) // 2
            dz = lax.rem(Z // 2 + lax.rem(k, 2) * (Z - 2 * back) + back, Z)
            send(plane(d) * Z + zline(dz))
            return c

        for d in order:
            lax.fori_loop(0, Z, functools.partial(step, d), 0)

    def rest(send):
        for d in z_order:
            send(xy * Z + zline(d))

    first, second = xy_order[:11], xy_order[11:]

    def send_bnd(p):
        remote(s1.at[p], br.at[r], 3, p, g).start()

    for d in z_order:
        remote(hown, h1.at[z], 0, xy * Z + zline(d), g).start()
    pltpu.make_async_copy(hown, h1.at[z], rsem.at[0]).start()

    loads["srows"].wait()

    def pack(i, c):
        for j in range(4):
            s1[i, pl.ds(j, 1), :] = feat[pl.ds(srows[j, i], 1), :]
        return c

    lax.fori_loop(0, R, pack, 0, unroll=4)
    load("bv", "hv", "cot")
    pltpu.make_async_copy(s1.at[r], br.at[r], rsem.at[3]).start()
    for d in xy_order:
        send_bnd(plane(d) * Z + z)

    for pair in range(1, Z // 2 + 1):
        for d in sorted({pair, Z - pair}):
            pl.semaphore_wait(plane_sem.at[zline(d)], 1)
        for dxy in xy_order + [(0, 0)]:
            for d in sorted({pair, Z - pair}):
                send_bnd(plane(dxy) * Z + zline(d))
    wait_recv(h1, 0)
    for d in xy_order:
        remote(h1, hub.at[g, pl.ds(xy * Z, Z)], 2, plane(d) * Z + z, g).start()
    pltpu.make_async_copy(h1, hub.at[g, pl.ds(xy * Z, Z)], rsem.at[2]).start()

    loads["lcols"].wait()
    loads["lcount"].wait()
    loads["lv"].wait()
    lane = lax.broadcasted_iota(jnp.int32, (TB, 2 * TB), 1)
    upper = lane >= TB
    for t in range(N // TB):
        rows = pl.ds(t * TB, TB)
        dup = []
        for pair in range(KT // 2):
            v = lv[rows, pl.ds(pair * 2 * TB, 2 * TB)]
            turned = pltpu.roll(v, TB, 1)
            dup.append(jnp.where(upper, turned, v))
            dup.append(jnp.where(upper, v, turned))
        cols = [jnp.where(k < lcount[0, t], lcols[k, t], -1) for k in range(KT)]
        for c in range(N // (2 * TB)):
            tile = jnp.where(upper, 2 * c + 1, 2 * c)
            out = jnp.zeros((TB, 2 * TB), F32)
            for k in range(KT):
                out = jnp.where(tile == cols[k], dup[k], out)
            high, low = split(out)
            ahi[rows, pl.ds(c * 2 * TB, 2 * TB)] = high
            alo[rows, pl.ds(c * 2 * TB, 2 * TB)] = low

    agg[...] = mm3(ahi[:, :N], alo[:, :N], wide(feat[...]))
    for c in range(N // 128):
        cols = pl.ds(c * 128, 128)
        athi[cols, :] = ahi[:, cols].astype(F32).T.astype(BF16)
        atlo[cols, :] = alo[:, cols].astype(F32).T.astype(BF16)

    loads["w"].wait()
    wv = w[...]
    wpair[...] = wide(wv)
    wt[...] = wide(wv.T)

    loads["bv"].wait()
    step = min(128, nb)
    for c in range(nb // step):
        v = bv[:, pl.ds(c * step, step)]
        high, low = split(v)
        ahi[:, pl.ds(N + c * step, step)] = high
        alo[:, pl.ds(N + c * step, step)] = low
        high, low = split(v.T)
        athi[pl.ds(N + c * step, step), :] = high
        atlo[pl.ds(N + c * step, step), :] = low

    loads["hv"].wait()
    step = min(128, nh)
    for c in range(nh // step):
        v = hv[:, pl.ds(c * step, step)]
        high, low = split(v)
        ahi[:, pl.ds(N + nb + c * step, step)] = high
        alo[:, pl.ds(N + nb + c * step, step)] = low
        turned = v.T.reshape(step // 8, 8, N)
        for core in range(2):
            high, low = split(turned[:, core * 4:core * 4 + 4, :].reshape(step // 2, N))
            to = pl.ds(N + nb + core * (nh // 2) + c * (step // 2), step // 2)
            athi[to, :] = high
            atlo[to, :] = low

    wait_recv(hub.at[g], 2)
    to_sib = remote(hub.at[g], hub.at[g], 4, r, 1 - g)
    to_sib.start()
    to_sib.wait_recv()
    vh = jnp.concatenate([hub[0], hub[1]], axis=1).reshape(nh, F)
    agg[...] += mm3(ahi[:, N + nb:], alo[:, N + nb:], wide(vh))
    wait_recv(br, 3)
    vb = br[...].reshape(nb, F)
    agg[...] += mm3(ahi[:, N:N + nb], alo[:, N:N + nb], wide(vb))

    loads["b"].wait()
    loads["cot"].wait()
    H = w.shape[1]
    step = 128
    wsplit = wpair[...]
    for c in range(N // step):
        rows = pl.ds(c * step, step)
        high, low = split(agg[rows, :])
        both = mm(high, wsplit)
        v = both[:, :H] + both[:, H:] + mm(low, wsplit[:, :H]) + b[...]
        sq = v * v
        t = jnp.tanh(C0 * (v + C1 * (sq * v)))
        act_o[rows, :] = 0.5 * v * (1.0 + t)
        slope = 0.5 * (1.0 + t) + 0.5 * v * (1.0 - t * t) * (C0 * (1.0 + 3.0 * C1 * sq))
        prg[rows, :] = cot[rows, :] * slope
    ahigh, alow = split(agg[...].T)
    wh, wl = split(prg[...])
    wterm = mm(ahigh, wh) + mm(ahigh, wl) + mm(alow, wh)
    ws[...] = jnp.concatenate([wterm[:, :F], wterm[:, F:]], axis=0).reshape(ws.shape)
    for d in xy_order:
        remote(ws.at[plane(d)], wx.at[xy], 8, plane(d) * Z + z, g).start()
    pltpu.make_async_copy(ws.at[xy], wx.at[xy], rsem.at[8]).start()

    high, low = split(prg[...])
    dag[...] = wide(mm3(high, low, wt[...]))

    g2 = dag[...]

    def back(start, size):
        return mm3(athi[pl.ds(start, size), :], atlo[pl.ds(start, size), :], g2)

    hbase = N + nb
    gs[...] = back(hbase + (1 - g) * (nh // 2), nh // 2)
    hub_sib = remote(gs, gsib, 5, r, 1 - g)
    hub_sib.start()
    own = back(hbase + g * (nh // 2), nh // 2)
    bsend[...] = back(N, nb).reshape(R, 4, F)
    hub_sib.wait_recv()
    gown[...] = (own + gsib[...]).reshape(XY, hb, F)
    for d in xy_order:
        remote(gown.at[plane(d)], gx.at[xy], 7, plane(d) * Z + z, g).start()
    pltpu.make_async_copy(gown.at[xy], gx.at[xy], rsem.at[7]).start()

    def send_back(p):
        remote(bsend.at[p], ar.at[r], 6, p, g).start()

    pltpu.make_async_copy(bsend.at[r], ar.at[r], rsem.at[6]).start()
    each(first, send_back)

    wait_recv(wx, 8)
    total = wx[0]
    for i in range(1, XY):
        total += wx[i]
    wp[0] = total
    w_sib = remote(wp.at[0], wsib, 12, r, 1 - g)
    w_sib.start()
    w_sib.wait_recv()
    wp[1] = total + wsib[...]
    for p in others(Z, z):
        remote(wp.at[1], wz.at[z], 11, xy * Z + p, g).start()
    pltpu.make_async_copy(wp.at[1], wz.at[z], rsem.at[11]).start()

    each(second, send_back)
    rest(send_back)

    fg_o[...] = back(0, N)

    wait_recv(gx, 7)
    total = gx[0]
    for i in range(1, XY):
        total += gx[i]
    gp[...] = total.reshape(Z, 4, F)
    for p in others(Z, z):
        remote(gp.at[p], gz.at[z], 10, xy * Z + p, g).start()
    pltpu.make_async_copy(gp.at[z], gz.at[z], rsem.at[10]).start()

    wait_recv(wz, 11)
    total = wz[0]
    for i in range(1, Z):
        total += wz[i]
    wsum[...] = total

    for p in others(XY, xy):
        remote(wsum, wall.at[xy], 13, p * Z + z, g).start()
    pltpu.make_async_copy(wsum, wall.at[xy], rsem.at[13]).start()

    loads["srows_v"].wait()
    node = lax.broadcasted_iota(jnp.int32, (N, R), 0)
    picks = [jnp.where(node == srows_v[pl.ds(j, 1), :], 1.0, 0.0).astype(BF16) for j in range(4)]
    pick = jnp.concatenate(picks, axis=1)
    wait_recv(ar, 6)
    arr = jnp.concatenate([ar[:, j, :] for j in range(4)], axis=0)
    both = mm(pick, wide(arr))
    fg_o[...] += both[:, :F] + both[:, F:]

    wait_recv(gz, 10)
    total = gz[0]
    for i in range(1, Z):
        total += gz[i]
    node = lax.broadcasted_iota(jnp.int32, (N, F), 0)
    for j in range(4):
        fg_o[...] += jnp.where(node == hrows[0, j], total[j:j + 1, :], 0.0)

    wait_recv(wall, 13)
    full = wall[...].reshape(2 * F, F) * float((R * 2 * N) ** -0.5)
    wg_o[:, :F] = full[:F]
    wg_o[:, F:] = full[F:]

    wait_send(h1.at[pl.ds(0, Z - 1)], 0)
    wait_send(hub.at[0, pl.ds(0, (XY - 1) * Z)], 2)
    wait_send(br.at[pl.ds(0, R - 1)], 3)
    to_sib.wait_send()
    hub_sib.wait_send()
    wait_send(ar.at[pl.ds(0, R - 1)], 6)
    wait_send(gown.at[pl.ds(0, XY - 1)], 7)
    wait_send(wx.at[pl.ds(0, XY - 1)], 8)

    wait_send(gz.at[pl.ds(0, Z - 1)], 10)
    wait_send(wz.at[pl.ds(0, Z - 1)], 11)
    w_sib.wait_send()
    wait_send(wall.at[pl.ds(0, XY - 1)], 13)


def write_out(a_ref, b_ref, c_ref, a_out, b_out, c_out, sems):
    copies = [
        pltpu.make_async_copy(a_ref, a_out, sems.at[0]),
        pltpu.make_async_copy(b_ref, b_out, sems.at[1]),
        pltpu.make_async_copy(c_ref, c_out, sems.at[2]),
    ]
    for copy in copies:
        copy.start()
    for copy in copies:
        copy.wait()


def shards(features, weight, bias, cotangent, loc_vals, loc_cols, loc_count, hub_rows, hub_vals, send_rows, bnd_vals):
    rows = lax.axis_size("rows")
    Z = 8 if rows % 8 == 0 else 2
    XY = rows // Z
    Y = 4 if XY % 4 == 0 else 1
    X = XY // Y
    N, F = features.shape
    H = weight.shape[1]
    nb = bnd_vals.shape[1]
    nh = hub_vals.shape[1]
    hb = Z * 4
    piece = 2 * F // XY
    K = N + nb + nh
    V = pltpu.VMEM
    D = pltpu.SemaphoreType.DMA
    hbm = pl.BlockSpec(memory_space=pltpu.HBM)
    vm = pl.BlockSpec(memory_space=pltpu.VMEM)
    scratch = [
        V((N, F), F32), V((F, H), F32), V((1, H), F32), V((N, H), F32), V((N, KT * TB), F32),
        pltpu.SMEM((KT, N // TB), jnp.int32), pltpu.SMEM((1, N // TB), jnp.int32),
        pltpu.SMEM((1, 4), jnp.int32),
        V((N, nh), F32), pltpu.SMEM((4, rows), jnp.int32), V((4, rows), jnp.int32), V((N, nb), F32),
        V((N, K), BF16), V((N, K), BF16), V((K, N), BF16), V((K, N), BF16),
        V((H, 2 * F), BF16), V((F, 2 * H), BF16),
        V((4, F), F32), V((rows, 4, F), F32), V((Z, 4, F), F32),
        V((rows, 4, F), F32), V((2, rows, 4, F), F32),
        V((N, F), F32), V((N, H), F32), V((N, 2 * F), BF16),
        V((nh // 2, F), F32), V((nh // 2, F), F32), V((XY, hb, F), F32), V((XY, hb, F), F32),
        V((Z, 4, F), F32), V((Z, 4, F), F32),
        V((rows, 4, F), F32), V((rows, 4, F), F32),
        V((XY, piece, F), F32), V((XY, piece, F), F32), V((2, piece, F), F32), V((piece, F), F32),
        V((Z, piece, F), F32), V((piece, F), F32), V((XY, piece, F), F32),
        D((12,)), D((14,)), D((14,)), pltpu.SemaphoreType.REGULAR((Z,)),
    ]
    results = pl.pallas_call(
        functools.partial(kernel, X, Y, Z),
        out_shape=(pltpu.VMEM((N, H), F32), pltpu.VMEM((F, H), F32), pltpu.VMEM((N, F), F32)),
        in_specs=[hbm] * 11,
        out_specs=(vm, vm, vm),
        scratch_shapes=scratch,
        compiler_params=pltpu.CompilerParams(
            collective_id=0, has_side_effects=True, vmem_limit_bytes=60 * 1024 * 1024
        ),
    )(
        features, weight, bias.reshape(1, H), cotangent, loc_vals, loc_cols.T,
        loc_count.reshape(1, -1), hub_rows.reshape(1, 4), hub_vals,
        send_rows[0].T, bnd_vals,
    )
    return pl.pallas_call(
        write_out,
        out_shape=(
            jax.ShapeDtypeStruct((N, H), F32),
            jax.ShapeDtypeStruct((F, H), F32),
            jax.ShapeDtypeStruct((N, F), F32),
        ),
        in_specs=[vm] * 3,
        out_specs=(pl.BlockSpec(memory_space=pl.ANY),) * 3,
        scratch_shapes=[D((3,))],
        compiler_params=pltpu.CompilerParams(vmem_limit_bytes=4 * 1024 * 1024),
    )(*results)


def solution(mesh):
    node = P(("rows", "grp"), None)
    flat = P(("rows", "grp"))
    return jax.shard_map(
        shards,
        mesh=mesh,
        in_specs=(node, P(), P(), node, node, node, flat, flat, node, P(("rows", "grp"), None, None), node),
        out_specs=(node, P(), node),
        check_vma=False,
    )
```
